256 devices in a mesh: space: 64 (over x, z, core), tm: 4 (over y).
Axes of the slice: x: 4, y: 4, z: 8, core: 2. Of those that a mesh axis runs over, the one named last changes fastest.
Arguments:
- previous: bfloat16 [64, 384, 256, 128], P('tm', 'space'), may hold values from 0 to 1
- initial: float32 [384, 256, 128], P('space'), may hold values from 0 to 1
- rates: float32 [384, 256], P('space'), may hold values from 0.005 to 0.3
- transitions: float32 [64, 128, 128], replicated, may hold values from -0.02 to 0.99, as said below
Outputs:
- trajectory: bfloat16 [64, 384, 256, 128], P('tm', 'space')
The draws below stay inside these ranges and needn't reach their ends.
Inputs may be any that keep to these rules, and one draw needn't show every extreme that they name: `transitions`: each matrix has its diagonal in 0.88 to 0.99 and small entries off it.
All inputs are finite; a program needn't handle non-finite values.
Results may differ from the reference program's by a relative error of at most 0.0015.
Values may be sent and summed in bfloat16 or wider, within the bound.
No kernel may reach another device: no remote copies, remote signals or barrier semaphores. Data moves between devices by JAX's collectives and lax.ppermute only.
A program may use at most 128 MiB of HBM per device.

```python
import math
import jax
import jax.numpy as jnp
from jax import lax

NC = 256
B = 128
NR = 384
NT = 64


def draw_transitions(key, part):
    key = jax.random.fold_in(key, 5)
    first, second = jax.random.split(key)
    stay = jax.random.uniform(first, (NT, B), jnp.float32, 0.88, 0.99)
    off = jnp.clip(jax.random.normal(second, (NT, B, B), jnp.float32) * (0.05 / B ** 0.5), -0.02, 0.02)
    eye = jnp.eye(B, dtype=jnp.float32)
    return off * (1.0 - eye)[None] + eye[None] * stay[:, :, None]


def steps_of(key, shape, cuts, smallest, top_value):
    factor_of, own = 1.0, jax.random.fold_in(key, 6)
    for dim, blocks in cuts:
        steps = jnp.exp(jax.random.uniform(jax.random.fold_in(own, dim), (blocks,), jnp.float32, smallest / len(cuts), top_value / len(cuts)))
        factor_of = factor_of * jnp.repeat(steps, shape[dim] // blocks).reshape([-1 if axis == dim else 1 for axis in range(len(shape))])
    return factor_of


def setup_inputs(seed: int = 0) -> dict:
    splits = jax.random.split(jax.random.key(seed), 5)
    return {
        "previous": jnp.clip(1.0 * jax.random.uniform(splits[0], (NT, NR, NC, B), jnp.float32) ** steps_of(splits[0], (NT, NR, NC, B), ((0, 4), (1, 64)), -0.2, 0.2), 0.0, 1.0).astype(jnp.bfloat16),
        "initial": jnp.clip(1.0 * jax.random.uniform(splits[1], (NR, NC, B), jnp.float32) ** steps_of(splits[1], (NR, NC, B), ((0, 64),), -0.2, 0.2), 0.0, 1.0),
        "rates": jnp.clip(jnp.exp(math.log(0.3) - 4.0943446 * jax.random.uniform(splits[2], (NR, NC), jnp.float32) ** steps_of(splits[2], (NR, NC), ((0, 64),), -0.2, 0.2)), 0.005, 0.3),
        "transitions": draw_transitions(jax.random.fold_in(splits[4], 71), 0),
    }


def neighbours(scaled):
    padded = jnp.pad(scaled, ((1, 1), (1, 1), (0, 0)))
    return padded[:-2, 1:-1] + padded[2:, 1:-1] + padded[1:-1, :-2] + padded[1:-1, 2:]


def reference(previous, initial, rates, transitions):
    keep = (1.0 - rates)[:, :, None]
    weight = (rates * 0.25)[:, :, None]

    def advance(state, inputs):
        old_step, matrix = inputs
        scaled = (old_step.astype(jnp.float32) * weight).astype(jnp.bfloat16)
        scaled = lax.optimization_barrier(scaled).astype(jnp.float32)
        mixed = keep * state + neighbours(scaled)
        state = jnp.einsum("rcb,bd->rcd", mixed, matrix, precision=lax.Precision.HIGHEST)
        return state, state.astype(jnp.bfloat16)

    final, states = lax.scan(advance, initial, (previous, transitions))
    return states
```

```python
import functools

import jax
import jax.numpy as jnp
from jax import lax
from jax.experimental import pallas as pl
from jax.experimental.pallas import tpu as pltpu
from jax.sharding import PartitionSpec as P

F32, BF16 = jnp.float32, jnp.bfloat16
PEAK = 2.0**15.5
CHUNK = 128
MIB = 1 << 20


def split(value):
    high = value.astype(BF16)
    low = (value - high.astype(F32)).astype(BF16)
    return high, low


def left(value):
    return jnp.concatenate(split(value), axis=1)


def right(matrix):
    both = jnp.concatenate(split(matrix), axis=1)
    return jnp.concatenate([both, both], axis=0)


def times(value, matrix):
    n = matrix.shape[1] // 2
    both = jnp.dot(left(value), matrix, preferred_element_type=F32)
    return both[:, :n] + both[:, n:]


def column(rates_ref, row, bins):
    line = rates_ref[pl.ds(row, 1), :]
    return jnp.broadcast_to(line, (bins, line.shape[1])).T


def place(q, rows, odd):
    return q + odd * (rows - 1 - 2 * q)


def encode(value, scale):
    u = value * (PEAK / scale)
    g = u * u
    g = g * g
    g = g * g
    return jnp.where(value < 0, -g, g).astype(BF16)


def decode(code, scale):
    g = code.astype(F32)
    root = jnp.exp(jnp.log(jnp.abs(g)) * 0.125) * (scale * (1.0 / PEAK))
    return jnp.where(g < 0, -root, root)


def sweep_kernel(
    own, calc, halo_q, steps, rows,
    prev_ref, halo_ref, init_ref, rates_ref, trans_ref,
    loc_ref, code_ref,
    pbuf, hbuf, ibuf, tbuf, grid, weight, keep, rhs, psem, hsem, isem, tsem,
):
    odd = lax.rem(lax.axis_index("space"), 2)
    block = lax.axis_index("tm")
    columns, bins = pbuf.shape[2], pbuf.shape[3]
    base = min(min(own), halo_q)
    whole = len(own) == rows

    def fetch(t):
        if whole:
            return [pltpu.make_async_copy(prev_ref.at[t], pbuf.at[t], psem.at[t])]
        return [
            pltpu.make_async_copy(prev_ref.at[t, place(q, rows, odd)], pbuf.at[t, i], psem.at[t])
            for i, q in enumerate(own)
        ]

    matrices = pltpu.make_async_copy(trans_ref.at[pl.ds(block * steps, steps)], tbuf, tsem)
    start = pltpu.make_async_copy(init_ref, ibuf, isem)
    halo = pltpu.make_async_copy(halo_ref, hbuf, hsem)
    matrices.start()
    start.start()
    for t in range(steps):
        for copy in fetch(t):
            copy.start()
    halo.start()

    for i, q in enumerate(own):
        share = column(rates_ref, place(q, rows, odd), bins)
        weight[i] = share * 0.25
        if q in calc:
            keep[q - calc[0]] = 1.0 - share
    for i in range(grid.shape[0]):
        grid[i, 0:8] = jnp.zeros((8, bins), F32)
        grid[i, columns + 8 : columns + 16] = jnp.zeros((8, bins), F32)
    matrices.wait()
    for t in range(steps):
        rhs[t] = right(tbuf[t])
    start.wait()
    for n, q in enumerate(calc):
        first = ibuf[place(q, rows, odd)]
        loc_ref[0, n] = jnp.where(block == 0, first, jnp.zeros_like(first))
    halo.wait()

    def step(t, carry):
        for copy in fetch(t):
            copy.wait()
        for i, q in enumerate(own):
            source = pbuf[t, place(q, rows, odd) if whole else i].astype(F32)
            grid[q - base, 8 : 8 + columns] = (source * weight[i]).astype(BF16).astype(F32)
        grid[halo_q - base, 8 : 8 + columns] = hbuf[t].astype(F32)
        matrix = rhs[t]
        for n, q in enumerate(calc):
            g = q - base
            for c in range(0, columns, CHUNK):
                at = slice(8 + c, 8 + c + CHUNK)
                inflow = (grid[g - 1, at] + grid[g + 1, at]) + (
                    grid[g, 7 + c : 7 + c + CHUNK] + grid[g, 9 + c : 9 + c + CHUNK]
                )
                cells = slice(c, c + CHUNK)
                mixed = keep[n, cells] * loc_ref[t, n, cells] + inflow
                loc_ref[t + 1, n, cells] = times(mixed, matrix)
        return carry

    lax.fori_loop(0, steps, step, 0)

    top = jnp.zeros((columns, bins), F32)
    for n in range(len(calc)):
        top = jnp.maximum(top, jnp.abs(loc_ref[steps, n]))
    scale = (jnp.max(top, keepdims=True) * 1.01 + 1e-30).astype(BF16).astype(F32)
    for n in range(len(calc)):
        code_ref[n * columns : (n + 1) * columns] = encode(loc_ref[steps, n], scale)
    code_ref[len(calc) * columns :] = jnp.broadcast_to(scale, (16, bins)).astype(BF16)


def sweep(previous, halo, initial, rates, transitions, own, calc, halo_q):
    steps, rows, columns, bins = previous.shape
    n = len(calc)
    anywhere = pl.BlockSpec(memory_space=pl.ANY)
    vmem = pl.BlockSpec(memory_space=pltpu.VMEM)
    return pl.pallas_call(
        functools.partial(sweep_kernel, own, calc, halo_q, steps, rows),
        out_shape=[
            pltpu.VMEM((steps + 1, n, columns, bins), F32),
            jax.ShapeDtypeStruct((n * columns + 16, bins), BF16),
        ],
        in_specs=[anywhere, anywhere, anywhere, vmem, anywhere],
        out_specs=[vmem, vmem],
        scratch_shapes=[
            pltpu.VMEM((steps, len(own), columns, bins), BF16),
            pltpu.VMEM((steps, columns, bins), BF16),
            pltpu.VMEM((rows, columns, bins), F32),
            pltpu.VMEM((steps, bins, bins), F32),
            pltpu.VMEM((len(own) + 1, columns + 16, bins), F32),
            pltpu.VMEM((len(own), columns, bins), F32),
            pltpu.VMEM((n, columns, bins), F32),
            pltpu.VMEM((steps, 2 * bins, 2 * bins), BF16),
            pltpu.SemaphoreType.DMA((steps,)),
            pltpu.SemaphoreType.DMA,
            pltpu.SemaphoreType.DMA,
            pltpu.SemaphoreType.DMA,
        ],
        compiler_params=pltpu.CompilerParams(vmem_limit_bytes=24 * MIB),
        cost_estimate=pl.CostEstimate(
            flops=8 * steps * n * columns * bins * bins,
            bytes_accessed=steps * len(own) * columns * bins * 2,
            transcendentals=0,
        ),
        name=f"sweep{n}",
    )(previous, halo, initial, rates, transitions)


def product_kernel(steps, trans_ref, prefix_ref, total_ref, tbuf, work, sems):
    block = lax.axis_index("tm")
    bins = tbuf.shape[2]
    copies = []
    for back in range(3):
        at = pl.ds(jnp.maximum(block - back, 0) * steps, steps)
        copies.append(
            pltpu.make_async_copy(
                trans_ref.at[at], tbuf.at[pl.ds(back * steps, steps)], sems.at[back]
            )
        )
        copies[-1].start()
    for copy in copies:
        copy.wait()
    for back in range(3):
        work[back] = tbuf[back * steps]
    prefix_ref[0] = right(tbuf[0])

    def step(t, carry):
        for back in range(3):
            work[back] = times(work[back], right(tbuf[back * steps + t]))
        prefix_ref[t] = right(work[0])
        return carry

    lax.fori_loop(1, steps, step, 0)
    total_ref[0] = right(work[1])
    total_ref[1] = right(work[2])


def products(transitions, steps):
    bins = transitions.shape[1]
    vmem = pl.BlockSpec(memory_space=pltpu.VMEM)
    return pl.pallas_call(
        functools.partial(product_kernel, steps),
        out_shape=[
            pltpu.VMEM((steps, 2 * bins, 2 * bins), BF16),
            pltpu.VMEM((2, 2 * bins, 2 * bins), BF16),
        ],
        in_specs=[pl.BlockSpec(memory_space=pl.ANY)],
        out_specs=[vmem, vmem],
        scratch_shapes=[
            pltpu.VMEM((3 * steps, bins, bins), F32),
            pltpu.VMEM((3, bins, bins), F32),
            pltpu.SemaphoreType.DMA((3,)),
        ],
        compiler_params=pltpu.CompilerParams(vmem_limit_bytes=16 * MIB),
        cost_estimate=pl.CostEstimate(
            flops=24 * steps * bins**3 * 4, bytes_accessed=4 * MIB, transcendentals=0
        ),
        name="products",
    )(transitions)


def spread_kernel(
    chunks, rows,
    a1_ref, b1_ref, c1_ref, a0_ref, b0_ref, c0_ref, loc1_ref, loc0_ref, rates_ref, prefix_ref, total_ref,
    out_ref,
    entering, keep, power, stage, sems,
):
    odd = lax.rem(lax.axis_index("space"), 2)
    steps, _, columns, bins = stage.shape
    codes = ((a1_ref, b1_ref, c1_ref), (a0_ref, b0_ref, c0_ref))
    locs = (loc1_ref, loc0_ref)

    for calc, refs in zip(chunks, codes):
        last = len(calc) * columns
        scales = [ref[last : last + 16].astype(F32)[0:1, 0:1] for ref in refs]
        for n, q in enumerate(calc):
            held = 1.0 - column(rates_ref, place(q, rows, odd), bins)
            keep[q] = held
            power[q] = jnp.ones_like(held)
            for _ in range(4):
                held = held * held
            at = slice(n * columns, (n + 1) * columns)
            near, mid, far = [decode(ref[at], scale) for ref, scale in zip(refs, scales)]
            state = mid + held * times(far, total_ref[1])
            state = near + held * times(state, total_ref[0])
            entering[q] = left(state)

    def step(t, carry):
        matrix = prefix_ref[t]
        for calc, loc_ref in zip(chunks, locs):
            for n, q in enumerate(calc):
                row = place(q, rows, odd)
                for c in range(0, columns, CHUNK):
                    cells = slice(c, c + CHUNK)
                    both = jnp.dot(entering[q, cells], matrix, preferred_element_type=F32)
                    factor = power[q, cells] * keep[q, cells]
                    power[q, cells] = factor
                    share = factor * (both[:, :bins] + both[:, bins:])
                    stage[t, row, cells] = (loc_ref[t + 1, n, cells] + share).astype(BF16)
        pltpu.make_async_copy(stage.at[t], out_ref.at[t], sems.at[t]).start()
        return carry

    lax.fori_loop(0, steps, step, 0)
    for t in range(steps):
        pltpu.make_async_copy(stage.at[t], out_ref.at[t], sems.at[t]).wait()


def spread(chunks, codes1, codes0, loc1, loc0, rates, prefix, total):
    steps, columns, bins = loc1.shape[0] - 1, loc1.shape[2], loc1.shape[3]
    rows = rates.shape[0]
    vmem = pl.BlockSpec(memory_space=pltpu.VMEM)
    return pl.pallas_call(
        functools.partial(spread_kernel, chunks, rows),
        out_shape=jax.ShapeDtypeStruct((steps, rows, columns, bins), BF16),
        in_specs=[vmem] * 11,
        out_specs=pl.BlockSpec(memory_space=pl.ANY),
        scratch_shapes=[
            pltpu.VMEM((rows, columns, 2 * bins), BF16),
            pltpu.VMEM((rows, columns, bins), F32),
            pltpu.VMEM((rows, columns, bins), F32),
            pltpu.VMEM((steps, rows, columns, bins), BF16),
            pltpu.SemaphoreType.DMA((steps,)),
        ],
        compiler_params=pltpu.CompilerParams(vmem_limit_bytes=24 * MIB),
        cost_estimate=pl.CostEstimate(
            flops=8 * steps * rows * columns * bins * bins,
            bytes_accessed=steps * rows * columns * bins * 2,
            transcendentals=0,
        ),
        name="spread",
    )(*codes1, *codes0, loc1, loc0, rates, prefix, total)


def local(previous, initial, rates, transitions):
    steps, rows, columns, bins = previous.shape
    strips, blocks = lax.axis_size("space"), lax.axis_size("tm")
    odd = lax.rem(lax.axis_index("space"), 2)

    def edge(row):
        taken = lax.dynamic_index_in_dim(previous, row, 1, False).astype(F32)
        share = lax.dynamic_index_in_dim(rates, row, 0, False) * 0.25
        return (taken * share[None, :, None]).astype(BF16)

    between = [(i, i + 1) for i in range(1, strips - 1, 2)]
    within = [(i, i + 1) for i in range(0, strips, 2)]
    outer = lax.ppermute(edge(place(0, rows, odd)), "space", between + [(j, i) for i, j in between])
    inner = lax.ppermute(edge(place(rows - 1, rows, odd)), "space", within + [(j, i) for i, j in within])

    def send(code):
        return [
            lax.ppermute(code, "tm", [(i, i + hop) for i in range(blocks - hop)])
            for hop in range(1, blocks)
        ]

    most, rest = tuple(range(1, rows)), (0,)
    loc1, code1 = sweep(previous, inner, initial, rates, transitions, tuple(range(rows)), most, rows)
    codes1 = send(code1)
    prefix, total = products(transitions, steps)
    loc0, code0 = sweep(previous, outer, initial, rates, transitions, (0, 1), rest, -1)
    codes0 = send(code0)
    return spread((most, rest), codes1, codes0, loc1, loc0, rates, prefix, total)


def solution(mesh):
    in_specs = (P("tm", "space", None, None), P("space", None, None), P("space", None), P())
    out_specs = P("tm", "space", None, None)
    return jax.shard_map(local, mesh=mesh, in_specs=in_specs, out_specs=out_specs, check_vma=False)
```

```python
import functools

import jax
import jax.numpy as jnp
from jax import lax
from jax.experimental import pallas as pl
from jax.experimental.pallas import tpu as pltpu
from jax.sharding import PartitionSpec as P

F32, BF16 = jnp.float32, jnp.bfloat16
PEAK = 2.0**15.5
CHUNK = 64
MIB = 1 << 20


def split(value):
    high = value.astype(BF16)
    low = (value - high.astype(F32)).astype(BF16)
    return high, low


def left(value):
    return jnp.concatenate(split(value), axis=1)


def right(matrix):
    both = jnp.concatenate(split(matrix), axis=1)
    return jnp.concatenate([both, both], axis=0)


def times(value, matrix):
    n = matrix.shape[1] // 2
    both = jnp.dot(left(value), matrix, preferred_element_type=F32)
    return both[:, :n] + both[:, n:]


def shares(rates_ref, which, bins):
    lines = [rates_ref[pl.ds(row, 1), :] for row in which]
    lines += [jnp.zeros_like(lines[0])] * (8 - len(lines))
    turned = jnp.concatenate(lines, axis=0).T
    return [jnp.broadcast_to(turned[:, i : i + 1], (turned.shape[0], bins)) for i in range(len(which))]


def place(q, rows, odd):
    return q + odd * (rows - 1 - 2 * q)


def encode(value, scale):
    u = value * (PEAK / scale)
    g = u * u
    g = g * g
    g = g * g
    return jnp.where(value < 0, -g, g).astype(BF16)


def decode(code, scale):
    g = code.astype(F32)
    root = jnp.exp(jnp.log(jnp.abs(g)) * 0.125) * (scale * (1.0 / PEAK))
    return jnp.where(g < 0, -root, root)


def stream(steps, count, matrix_of, left_of, store, beside=None):
    lag = max(n for n in range(2, 13, 2) if count % n == 0)

    def push(t):
        matrix = matrix_of(t)
        pltpu.matmul_push_rhs(matrix, 0, 0)
        pltpu.matmul_push_rhs(matrix, 0, 1)

    def run(*accs):
        def emit(t, first, last, slot):
            for i in range(count):
                acc = accs[i % lag]
                if i >= lag:
                    store(t, i - lag, pltpu.matmul_pop(acc))
                elif not first:
                    store(t - 1, count - lag + i, pltpu.matmul_pop(acc))
                pltpu.matmul_acc_lhs(acc, left_of(t, i, slot), load_staged_rhs=0 if i < 2 else None)
                if i == 1 and not last:
                    push(t + 1)
                if beside is not None:
                    beside(t, i, slot)

        push(0)
        emit(0, True, steps == 1, 0)

        def pair(k, carry):
            emit(2 * k + 1, False, False, 1)
            emit(2 * k + 2, False, False, 0)
            return carry

        pairs = max(steps - 2, 0) // 2
        lax.fori_loop(0, pairs, pair, 0)
        for t in range(2 * pairs + 1, steps):
            emit(t, False, t == steps - 1, t % 2)
        for i in range(lag):
            store(steps - 1, count - lag + i, pltpu.matmul_pop(accs[i]))

    pl.run_scoped(run, *[pltpu.ACC(i % 2)((CHUNK, 256), F32) for i in range(lag)])


def halves(both):
    n = both.shape[1] // 2
    return both[:, :n] + both[:, n:]


def finish(loc_ref, code_ref, steps):
    rows, columns, bins = loc_ref.shape[1:]
    top = jnp.zeros((columns, bins), F32)
    for n in range(rows):
        top = jnp.maximum(top, jnp.abs(loc_ref[steps - 1, n]))
    scale = (jnp.max(top, keepdims=True) * 1.01 + 1e-30).astype(BF16).astype(F32)
    for n in range(rows):
        code_ref[n * columns : (n + 1) * columns] = encode(loc_ref[steps - 1, n], scale)
    code_ref[rows * columns :] = jnp.broadcast_to(scale, (16, bins)).astype(BF16)


def edge_kernel(steps, rows, prev_ref, line_ref, outer_ref, inner_ref, buf, rates_ref, sems, rsem):
    odd = lax.rem(lax.axis_index("space"), 2)
    bins = buf.shape[3]
    order = [place(0, rows, odd), place(rows - 1, rows, odd)]
    group = steps // sems.shape[1]

    def fetch(side, k):
        at = pl.ds(k * group, group)
        return pltpu.make_async_copy(
            prev_ref.at[at, order[side]], buf.at[side, at], sems.at[side, k]
        )

    parts = [(side, k) for side in range(2) for k in range(sems.shape[1])]
    lines = pltpu.make_async_copy(line_ref, rates_ref, rsem)
    lines.start()
    for part in parts:
        fetch(*part).start()
    lines.wait()
    weights = [share * 0.25 for share in shares(rates_ref, order, bins)]
    for side, k in parts:
        fetch(side, k).wait()
        out_ref = (outer_ref, inner_ref)[side]
        for t in range(k * group, (k + 1) * group):
            out_ref[t] = (buf[side, t].astype(F32) * weights[side]).astype(BF16)


def edges(previous, rates):
    steps, rows, columns, bins = previous.shape
    vmem = pl.BlockSpec(memory_space=pltpu.VMEM)
    return pl.pallas_call(
        functools.partial(edge_kernel, steps, rows),
        out_shape=[jax.ShapeDtypeStruct((steps, columns, bins), BF16)] * 2,
        in_specs=[pl.BlockSpec(memory_space=pl.ANY)] * 2,
        out_specs=[vmem] * 2,
        scratch_shapes=[
            pltpu.VMEM((2, steps, columns, bins), BF16),
            pltpu.VMEM((rows, columns), F32),
            pltpu.SemaphoreType.DMA((2, 4)),
            pltpu.SemaphoreType.DMA,
        ],
        compiler_params=pltpu.CompilerParams(vmem_limit_bytes=8 * MIB),
        cost_estimate=pl.CostEstimate(flops=0, bytes_accessed=0, transcendentals=0),
        name="edges",
    )(*[pltpu.with_memory_space_constraint(a, pltpu.HBM) for a in (previous, rates)])


def inner_kernel(
    steps, rows,
    prev_ref, halo_ref, init_ref, line_ref, trans_ref,
    loc_ref, code_ref, part_ref, first_ref, keep_ref, rhs_ref,
    pbuf, ibuf, tbuf, even, odds, weight, state, rates_ref, psem, isem, tsem, rsem,
):
    odd = lax.rem(lax.axis_index("space"), 2)
    block = lax.axis_index("tm")
    columns, bins = pbuf.shape[2], pbuf.shape[3]

    def fetch(t):
        return pltpu.make_async_copy(prev_ref.at[t], pbuf.at[t], psem.at[t])

    matrices = pltpu.make_async_copy(trans_ref.at[pl.ds(block * steps, steps)], tbuf, tsem)
    start = pltpu.make_async_copy(init_ref, ibuf, isem)
    lines = pltpu.make_async_copy(line_ref, rates_ref, rsem)
    lines.start()
    matrices.start()
    start.start()
    for t in range(steps):
        fetch(t).start()
    lines.wait()
    for q, share in enumerate(shares(rates_ref, [place(q, rows, odd) for q in range(rows)], bins)):
        weight[q] = share * 0.25
        keep_ref[q] = 1.0 - share
    grids = (even, odds)
    for grid in grids:
        for i in range(rows + 1):
            grid[i, 0:8] = jnp.zeros((8, bins), F32)
            grid[i, columns + 8 :] = jnp.zeros((8, bins), F32)
    matrices.wait()
    for t in range(steps):
        rhs_ref[t] = right(tbuf[t])
    start.wait()
    for q in range(rows):
        value = ibuf[place(q, rows, odd)]
        value = jnp.where(block == 0, value, jnp.zeros_like(value))
        if q == 0:
            first_ref[...] = value
        else:
            state[q - 1] = value

    pieces = [(q, c) for q in range(1, rows) for c in range(0, columns, CHUNK)]

    units = [(q, c) for q in range(rows + 1) for c in range(0, columns, CHUNK)]

    def fill(t, unit, slot):
        q, c = unit
        if q == rows:
            value = halo_ref[t, c : c + CHUNK].astype(F32)
        else:
            value = pbuf[t, place(q, rows, odd), c : c + CHUNK].astype(F32)
            value = (value * weight[q, c : c + CHUNK]).astype(BF16).astype(F32)
        grids[slot][q, 8 + c : 8 + c + CHUNK] = value

    def sides(grid, q, c):
        return grid[q, 7 + c : 7 + c + CHUNK] + grid[q, 9 + c : 9 + c + CHUNK]

    def left_of(t, i, slot):
        q, c = pieces[i]
        grid, inside, cells = grids[slot], slice(8 + c, 8 + c + CHUNK), slice(c, c + CHUNK)
        inflow = (grid[q - 1, inside] + grid[q + 1, inside]) + sides(grid, q, c)
        return left(keep_ref[q, cells] * state[q - 1, cells] + inflow)

    def store(t, i, both):
        q, c = pieces[i]
        value = halves(both)
        state[q - 1, c : c + CHUNK] = value
        loc_ref[t, q - 1, c : c + CHUNK] = value

    def beside(t, i, slot):
        if i % rows == 0 and i // rows < columns // CHUNK:
            c = i // rows * CHUNK
            grid = grids[slot]
            part_ref[t, c : c + CHUNK] = grid[1, 8 + c : 8 + c + CHUNK] + sides(grid, 0, c)
        if isinstance(t, int) and t == steps - 1:
            return
        if i == 0:
            fetch(t + 1).wait()
        for unit in units[len(units) * i // len(pieces) : len(units) * (i + 1) // len(pieces)]:
            fill(t + 1, unit, 1 - slot)

    fetch(0).wait()
    for unit in units:
        fill(0, unit, 0)
    stream(steps, len(pieces), lambda t: rhs_ref[t], left_of, store, beside)
    finish(loc_ref, code_ref, steps)


def inner_rows(previous, halo, initial, rates, transitions):
    steps, rows, columns, bins = previous.shape
    anywhere = pl.BlockSpec(memory_space=pl.ANY)
    vmem = pl.BlockSpec(memory_space=pltpu.VMEM)
    previous, initial, rates, transitions = [
        pltpu.with_memory_space_constraint(a, pltpu.HBM)
        for a in (previous, initial, rates, transitions)
    ]
    return pl.pallas_call(
        functools.partial(inner_kernel, steps, rows),
        out_shape=[
            pltpu.VMEM((steps, rows - 1, columns, bins), F32),
            jax.ShapeDtypeStruct(((rows - 1) * columns + 16, bins), BF16),
            pltpu.VMEM((steps, columns, bins), F32),
            pltpu.VMEM((columns, bins), F32),
            pltpu.VMEM((rows, columns, bins), F32),
            pltpu.VMEM((steps, 2 * bins, 2 * bins), BF16),
        ],
        in_specs=[anywhere, vmem, anywhere, anywhere, anywhere],
        out_specs=[vmem] * 6,
        scratch_shapes=[
            pltpu.VMEM((steps, rows, columns, bins), BF16),
            pltpu.VMEM((rows, columns, bins), F32),
            pltpu.VMEM((steps, bins, bins), F32),
            pltpu.VMEM((rows + 1, columns + 16, bins), F32),
            pltpu.VMEM((rows + 1, columns + 16, bins), F32),
            pltpu.VMEM((rows, columns, bins), F32),
            pltpu.VMEM((rows - 1, columns, bins), F32),
            pltpu.VMEM((rows, columns), F32),
            pltpu.SemaphoreType.DMA((steps,)),
            pltpu.SemaphoreType.DMA,
            pltpu.SemaphoreType.DMA,
            pltpu.SemaphoreType.DMA,
        ],
        compiler_params=pltpu.CompilerParams(vmem_limit_bytes=16 * MIB),
        cost_estimate=pl.CostEstimate(
            flops=8 * steps * rows * columns * bins * bins,
            bytes_accessed=steps * rows * columns * bins * 2,
            transcendentals=0,
        ),
        name="inner_rows",
    )(previous, halo, initial, rates, transitions)


def outer_kernel(
    steps, halo_ref, part_ref, first_ref, keep_ref, rhs_ref, most_ref, loc_ref, code_ref, all_ref, state, sem
):
    columns = first_ref.shape[0]
    joined = most_ref.shape[0]
    copy = pltpu.make_async_copy(most_ref, all_ref.at[pl.ds(0, joined)], sem)
    copy.start()
    state[...] = first_ref[...]

    def left_of(t, i, _):
        cells = slice(i * CHUNK, (i + 1) * CHUNK)
        inflow = part_ref[t, cells] + halo_ref[t, cells].astype(F32)
        return left(keep_ref[0, cells] * state[cells] + inflow)

    def store(t, i, both):
        cells = slice(i * CHUNK, (i + 1) * CHUNK)
        state[cells] = loc_ref[t, 0, cells] = halves(both)

    stream(steps, columns // CHUNK, lambda t: rhs_ref[t], left_of, store)
    finish(loc_ref, code_ref, steps)
    all_ref[joined:] = code_ref[...]
    copy.wait()


def outer_row(halo, part, first, keep, rhs, most):
    steps, columns, bins = part.shape
    vmem = pl.BlockSpec(memory_space=pltpu.VMEM)
    return pl.pallas_call(
        functools.partial(outer_kernel, steps),
        out_shape=[
            pltpu.VMEM((steps, 1, columns, bins), F32),
            jax.ShapeDtypeStruct((columns + 16, bins), BF16),
            jax.ShapeDtypeStruct((most.shape[0] + columns + 16, bins), BF16),
        ],
        in_specs=[vmem] * 6,
        out_specs=[vmem] * 3,
        scratch_shapes=[pltpu.VMEM((columns, bins), F32), pltpu.SemaphoreType.DMA],
        compiler_params=pltpu.CompilerParams(vmem_limit_bytes=4 * MIB),
        cost_estimate=pl.CostEstimate(
            flops=0, bytes_accessed=0, transcendentals=0
        ),
        name="outer_row",
    )(halo, part, first, keep, rhs, most)


def product_kernel(steps, trans_ref, prefix_ref, total_ref, tbuf, work, sems):
    block = lax.axis_index("tm")
    bins = tbuf.shape[2]
    copies = []
    for back in range(3):
        at = pl.ds(jnp.maximum(block - back, 0) * steps, steps)
        copies.append(
            pltpu.make_async_copy(
                trans_ref.at[at], tbuf.at[pl.ds(back * steps, steps)], sems.at[back]
            )
        )
        copies[-1].start()
    for copy in copies:
        copy.wait()
    for back in range(3):
        work[back] = tbuf[back * steps]
    prefix_ref[0] = right(tbuf[0])

    def step(t, carry):
        for back in range(3):
            work[back] = times(work[back], right(tbuf[back * steps + t]))
        prefix_ref[t] = right(work[0])
        return carry

    lax.fori_loop(1, steps, step, 0)
    total_ref[0] = right(work[1])
    total_ref[1] = right(work[2])


def products(transitions, steps):
    bins = transitions.shape[1]
    transitions = pltpu.with_memory_space_constraint(transitions, pltpu.HBM)
    vmem = pl.BlockSpec(memory_space=pltpu.VMEM)
    return pl.pallas_call(
        functools.partial(product_kernel, steps),
        out_shape=[
            pltpu.VMEM((steps, 2 * bins, 2 * bins), BF16),
            pltpu.VMEM((2, 2 * bins, 2 * bins), BF16),
        ],
        in_specs=[pl.BlockSpec(memory_space=pl.ANY)],
        out_specs=[vmem, vmem],
        scratch_shapes=[
            pltpu.VMEM((3 * steps, bins, bins), F32),
            pltpu.VMEM((3, bins, bins), F32),
            pltpu.SemaphoreType.DMA((3,)),
        ],
        compiler_params=pltpu.CompilerParams(vmem_limit_bytes=16 * MIB),
        cost_estimate=pl.CostEstimate(
            flops=0, bytes_accessed=0, transcendentals=0
        ),
        name="products",
    )(transitions)


def scale_of(ref, last):
    return ref[last : last + 16].astype(F32)[0:1, 0:1]


def decay(held):
    for _ in range(4):
        held = held * held
    return held


def ready_kernel(
    chunks, near1_ref, near0_ref, far1_ref, far0_ref, keep_ref, total_ref, near_ref, far_ref
):
    columns = keep_ref.shape[1]
    pieces = [(k, n, q, c) for k, calc in enumerate(chunks) for n, q in enumerate(calc) for c in range(0, columns, CHUNK)]
    refs = ((near1_ref, far1_ref), (near0_ref, far0_ref))
    scales = [[scale_of(ref, len(calc) * columns) for ref in pair] for calc, pair in zip(chunks, refs)]

    def carried(i, which):
        k, n, _, c = pieces[i]
        at = n * columns + c
        return decode(refs[k][which][at : at + CHUNK], scales[k][which])

    def store(_, i, both):
        _, _, q, c = pieces[i]
        cells = slice(c, c + CHUNK)
        near_ref[q, cells] = carried(i, 0)
        far_ref[q, cells] = decay(keep_ref[q, cells]) * halves(both)

    stream(1, len(pieces), lambda _: total_ref[1], lambda _, i, s: left(carried(i, 1)), store)


def ready(chunks, codes, keep, total):
    vmem = pl.BlockSpec(memory_space=pltpu.VMEM)
    return pl.pallas_call(
        functools.partial(ready_kernel, chunks),
        out_shape=[pltpu.VMEM(keep.shape, F32)] * 2,
        in_specs=[vmem] * 6,
        out_specs=[vmem] * 2,
        compiler_params=pltpu.CompilerParams(vmem_limit_bytes=4 * MIB),
        cost_estimate=pl.CostEstimate(flops=4000000000, bytes_accessed=8000000, transcendentals=0),
        name="ready",
    )(*codes, keep, total)


def spread_kernel(
    chunks, rows,
    near_ref, far_ref, mid_ref, loc1_ref, loc0_ref, keep_ref, prefix_ref, total_ref,
    out_ref,
    entering, power, stage, sems,
):
    odd = lax.rem(lax.axis_index("space"), 2)
    steps, _, columns, bins = stage.shape
    locs = (loc1_ref, loc0_ref)
    pieces, at, scales = [], 0, []
    for k, calc in enumerate(chunks):
        for n, q in enumerate(calc):
            pieces += [(k, n, q, c, at + c) for c in range(0, columns, CHUNK)]
            at += columns
        scales.append(scale_of(mid_ref, at))
        at += 16
    count = len(pieces)

    def cells_of(i):
        return pieces[i][2], slice(pieces[i][3], pieces[i][3] + CHUNK)

    def left_mid(_, i, slot):
        k, n, q, c, at = pieces[i]
        return left(decode(mid_ref[at : at + CHUNK], scales[k]) + far_ref[cells_of(i)])

    def store_mid(_, i, both):
        state = near_ref[cells_of(i)] + decay(keep_ref[cells_of(i)]) * halves(both)
        entering[cells_of(i)] = left(state)
        power[cells_of(i)] = jnp.ones((CHUNK, bins), F32)

    stream(1, count, lambda _: total_ref[0], left_mid, store_mid)

    def store(t, i, both):
        k, n, q, c, _ = pieces[i]
        factor = power[cells_of(i)] * keep_ref[cells_of(i)]
        power[cells_of(i)] = factor
        value = locs[k][t, n, c : c + CHUNK] + factor * halves(both)
        stage[t, place(q, rows, odd), c : c + CHUNK] = value.astype(BF16)
        if i == count - 1:
            pltpu.make_async_copy(stage.at[t], out_ref.at[t], sems.at[t]).start()

    stream(steps, count, lambda t: prefix_ref[t], lambda t, i, slot: entering[cells_of(i)], store)
    for t in range(steps):
        pltpu.make_async_copy(stage.at[t], out_ref.at[t], sems.at[t]).wait()


def spread(chunks, near, far, mid, loc1, loc0, keep, prefix, total):
    steps, _, columns, bins = loc1.shape
    rows = keep.shape[0]
    vmem = pl.BlockSpec(memory_space=pltpu.VMEM)
    return pl.pallas_call(
        functools.partial(spread_kernel, chunks, rows),
        out_shape=jax.ShapeDtypeStruct((steps, rows, columns, bins), BF16),
        in_specs=[vmem] * 8,
        out_specs=pl.BlockSpec(memory_space=pl.ANY),
        scratch_shapes=[
            pltpu.VMEM((rows, columns, 2 * bins), BF16),
            pltpu.VMEM((rows, columns, bins), F32),
            pltpu.VMEM((steps, rows, columns, bins), BF16),
            pltpu.SemaphoreType.DMA((steps,)),
        ],
        compiler_params=pltpu.CompilerParams(vmem_limit_bytes=16 * MIB),
        cost_estimate=pl.CostEstimate(
            flops=8 * steps * rows * columns * bins * bins,
            bytes_accessed=steps * rows * columns * bins * 2,
            transcendentals=0,
        ),
        name="spread",
    )(near, far, mid, loc1, loc0, keep, prefix, total)


def local(previous, initial, rates, transitions):
    steps, rows, columns, bins = previous.shape
    strips, blocks = lax.axis_size("space"), lax.axis_size("tm")
    outer_edge, inner_edge = edges(previous, rates)
    between = [(i, i + 1) for i in range(1, strips - 1, 2)]
    within = [(i, i + 1) for i in range(0, strips, 2)]
    outer = lax.ppermute(outer_edge, "space", between + [(j, i) for i, j in between])
    inner = lax.ppermute(inner_edge, "space", within + [(j, i) for i, j in within])

    def send(code, hop):
        return lax.ppermute(code, "tm", [(i, i + hop) for i in range(blocks - hop)])

    most, rest = tuple(range(1, rows)), (0,)
    loc1, code1, part, first, keep, rhs = inner_rows(previous, inner, initial, rates, transitions)
    near1, far1 = send(code1, 1), send(code1, 3)
    loc0, code0, code = outer_row(outer, part, first, keep, rhs, code1)
    mid, near0, far0 = send(code, 2), send(code0, 1), send(code0, 3)
    prefix, total = products(transitions, steps)
    chunks = (most, rest)
    near, far = ready(chunks, [near1, near0, far1, far0], keep, total)
    return spread(chunks, near, far, mid, loc1, loc0, keep, prefix, total)


def solution(mesh):
    in_specs = (P("tm", "space", None, None), P("space", None, None), P("space", None), P())
    out_specs = P("tm", "space", None, None)
    return jax.shard_map(local, mesh=mesh, in_specs=in_specs, out_specs=out_specs, check_vma=False)
```

```python
import functools

import jax
import jax.numpy as jnp
from jax import lax
from jax.experimental import pallas as pl
from jax.experimental.pallas import tpu as pltpu
from jax.sharding import PartitionSpec as P

F32, BF16 = jnp.float32, jnp.bfloat16
PEAK = 2.0**15.5
CHUNK = 64
MIB = 1 << 20


def split(value):
    high = value.astype(BF16)
    low = (value - high.astype(F32)).astype(BF16)
    return high, low


def left(value):
    return jnp.concatenate(split(value), axis=1)


def right(matrix):
    both = jnp.concatenate(split(matrix), axis=1)
    return jnp.concatenate([both, both], axis=0)


def times(value, matrix):
    n = matrix.shape[1] // 2
    both = jnp.dot(left(value), matrix, preferred_element_type=F32)
    return both[:, :n] + both[:, n:]


def shares(rates_ref, which, bins):
    lines = [rates_ref[pl.ds(row, 1), :] for row in which]
    lines += [jnp.zeros_like(lines[0])] * (8 - len(lines))
    turned = jnp.concatenate(lines, axis=0).T
    return [jnp.broadcast_to(turned[:, i : i + 1], (turned.shape[0], bins)) for i in range(len(which))]


def place(q, rows, odd):
    return q + odd * (rows - 1 - 2 * q)


def encode(value, scale):
    u = value * (PEAK / scale)
    g = u * u
    g = g * g
    g = g * g
    return jnp.where(value < 0, -g, g).astype(BF16)


def decode(code, scale):
    g = code.astype(F32)
    root = jnp.exp(jnp.log(jnp.abs(g)) * 0.125) * (scale * (1.0 / PEAK))
    return jnp.where(g < 0, -root, root)


def stream(steps, count, matrix_of, left_of, store, beside=None):
    lag = max(n for n in range(2, 13, 2) if count % n == 0)

    def push(t):
        matrix = matrix_of(t)
        pltpu.matmul_push_rhs(matrix, 0, 0)
        pltpu.matmul_push_rhs(matrix, 0, 1)

    def run(*accs):
        def emit(t, first, last, slot):
            for i in range(count):
                acc = accs[i % lag]
                if i >= lag:
                    store(t, i - lag, pltpu.matmul_pop(acc))
                elif not first:
                    store(t - 1, count - lag + i, pltpu.matmul_pop(acc))
                pltpu.matmul_acc_lhs(acc, left_of(t, i, slot), load_staged_rhs=0 if i < 2 else None)
                if i == count // 2 and not last:
                    push(t + 1)
                if beside is not None:
                    beside(t, i, slot)

        push(0)
        emit(0, True, steps == 1, 0)

        def pair(k, carry):
            emit(2 * k + 1, False, False, 1)
            emit(2 * k + 2, False, False, 0)
            return carry

        pairs = max(steps - 2, 0) // 2
        lax.fori_loop(0, pairs, pair, 0)
        for t in range(2 * pairs + 1, steps):
            emit(t, False, t == steps - 1, t % 2)
        for i in range(lag):
            store(steps - 1, count - lag + i, pltpu.matmul_pop(accs[i]))

    pl.run_scoped(run, *[pltpu.ACC(i % 2)((CHUNK, 256), F32) for i in range(lag)])


def halves(both):
    n = both.shape[1] // 2
    return both[:, :n] + both[:, n:]


def finish(loc_ref, code_ref, steps):
    rows, columns, bins = loc_ref.shape[1:]
    top = jnp.zeros((columns, bins), F32)
    for n in range(rows):
        top = jnp.maximum(top, jnp.abs(loc_ref[steps - 1, n]))
    scale = (jnp.max(top, keepdims=True) * 1.01 + 1e-30).astype(BF16).astype(F32)
    for n in range(rows):
        code_ref[n * columns : (n + 1) * columns] = encode(loc_ref[steps - 1, n], scale)
    code_ref[rows * columns :] = jnp.broadcast_to(scale, (16, bins)).astype(BF16)


def edge_kernel(steps, rows, prev_ref, line_ref, outer_ref, inner_ref, buf, rates_ref, sems, rsem):
    odd = lax.rem(lax.axis_index("space"), 2)
    bins = buf.shape[3]
    order = [place(0, rows, odd), place(rows - 1, rows, odd)]
    group = steps // sems.shape[1]

    def fetch(side, k):
        at = pl.ds(k * group, group)
        return pltpu.make_async_copy(
            prev_ref.at[at, order[side]], buf.at[side, at], sems.at[side, k]
        )

    parts = [(side, k) for side in range(2) for k in range(sems.shape[1])]
    lines = pltpu.make_async_copy(line_ref, rates_ref, rsem)
    lines.start()
    for part in parts:
        fetch(*part).start()
    lines.wait()
    weights = [share * 0.25 for share in shares(rates_ref, order, bins)]
    for side, k in parts:
        fetch(side, k).wait()
        out_ref = (outer_ref, inner_ref)[side]
        for t in range(k * group, (k + 1) * group):
            out_ref[t] = (buf[side, t].astype(F32) * weights[side]).astype(BF16)


def edges(previous, rates):
    steps, rows, columns, bins = previous.shape
    vmem = pl.BlockSpec(memory_space=pltpu.VMEM)
    return pl.pallas_call(
        functools.partial(edge_kernel, steps, rows),
        out_shape=[jax.ShapeDtypeStruct((steps, columns, bins), BF16)] * 2,
        in_specs=[pl.BlockSpec(memory_space=pl.ANY)] * 2,
        out_specs=[vmem] * 2,
        scratch_shapes=[
            pltpu.VMEM((2, steps, columns, bins), BF16),
            pltpu.VMEM((rows, columns), F32),
            pltpu.SemaphoreType.DMA((2, 4)),
            pltpu.SemaphoreType.DMA,
        ],
        compiler_params=pltpu.CompilerParams(vmem_limit_bytes=8 * MIB),
        cost_estimate=pl.CostEstimate(flops=0, bytes_accessed=0, transcendentals=0),
        name="edges",
    )(*[pltpu.with_memory_space_constraint(a, pltpu.HBM) for a in (previous, rates)])


def inner_kernel(
    steps, rows,
    prev_ref, halo_ref, init_ref, line_ref, trans_ref,
    loc_ref, code_ref, part_ref, first_ref, keep_ref, rhs_ref,
    pbuf, ibuf, tbuf, even, odds, weight, state, rates_ref, psem, isem, tsem, rsem,
):
    odd = lax.rem(lax.axis_index("space"), 2)
    block = lax.axis_index("tm")
    columns, bins = pbuf.shape[2], pbuf.shape[3]

    def fetch(t):
        return pltpu.make_async_copy(prev_ref.at[t], pbuf.at[t], psem.at[t])

    def matrix(t):
        return pltpu.make_async_copy(trans_ref.at[block * steps + t], tbuf.at[t], tsem.at[t])

    start = pltpu.make_async_copy(init_ref, ibuf, isem)
    lines = pltpu.make_async_copy(line_ref, rates_ref, rsem)
    lines.start()
    matrix(0).start()
    fetch(0).start()
    start.start()
    lines.wait()
    for q, share in enumerate(shares(rates_ref, [place(q, rows, odd) for q in range(rows)], bins)):
        weight[q] = share * 0.25
        keep_ref[q] = 1.0 - share
    grids = (even, odds)
    for grid in grids:
        for i in range(rows + 1):
            grid[i, 0:8] = jnp.zeros((8, bins), F32)
            grid[i, columns + 8 :] = jnp.zeros((8, bins), F32)
    for t in range(1, steps):
        matrix(t).start()
        fetch(t).start()
    matrix(0).wait()
    rhs_ref[0] = right(tbuf[0])
    start.wait()
    for q in range(rows):
        value = ibuf[place(q, rows, odd)]
        value = jnp.where(block == 0, value, jnp.zeros_like(value))
        if q == 0:
            first_ref[...] = value
        else:
            state[q - 1] = value

    pieces = [(q, c) for q in range(1, rows) for c in range(0, columns, CHUNK)]

    units = [(q, c) for q in range(rows + 1) for c in range(0, columns, CHUNK)]

    def fill(t, unit, slot):
        q, c = unit
        if q == rows:
            value = halo_ref[t, c : c + CHUNK].astype(F32)
        else:
            value = pbuf[t, place(q, rows, odd), c : c + CHUNK].astype(F32)
            value = (value * weight[q, c : c + CHUNK]).astype(BF16).astype(F32)
        grids[slot][q, 8 + c : 8 + c + CHUNK] = value

    def sides(grid, q, c):
        return grid[q, 7 + c : 7 + c + CHUNK] + grid[q, 9 + c : 9 + c + CHUNK]

    def left_of(t, i, slot):
        q, c = pieces[i]
        grid, inside, cells = grids[slot], slice(8 + c, 8 + c + CHUNK), slice(c, c + CHUNK)
        inflow = (grid[q - 1, inside] + grid[q + 1, inside]) + sides(grid, q, c)
        return left(keep_ref[q, cells] * state[q - 1, cells] + inflow)

    def store(t, i, both):
        q, c = pieces[i]
        value = halves(both)
        state[q - 1, c : c + CHUNK] = value
        loc_ref[t, q - 1, c : c + CHUNK] = value

    def beside(t, i, slot):
        if i % rows == 0 and i // rows < columns // CHUNK:
            c = i // rows * CHUNK
            grid = grids[slot]
            part_ref[t, c : c + CHUNK] = grid[1, 8 + c : 8 + c + CHUNK] + sides(grid, 0, c)
        if isinstance(t, int) and t == steps - 1:
            return
        if i == 0:
            fetch(t + 1).wait()
        if i == 2:
            matrix(t + 1).wait()
            rhs_ref[t + 1] = right(tbuf[t + 1])
        for unit in units[len(units) * i // len(pieces) : len(units) * (i + 1) // len(pieces)]:
            fill(t + 1, unit, 1 - slot)

    fetch(0).wait()
    for unit in units:
        fill(0, unit, 0)
    stream(steps, len(pieces), lambda t: rhs_ref[t], left_of, store, beside)
    finish(loc_ref, code_ref, steps)


def inner_rows(previous, halo, initial, rates, transitions):
    steps, rows, columns, bins = previous.shape
    anywhere = pl.BlockSpec(memory_space=pl.ANY)
    vmem = pl.BlockSpec(memory_space=pltpu.VMEM)
    previous, initial, rates, transitions = [
        pltpu.with_memory_space_constraint(a, pltpu.HBM)
        for a in (previous, initial, rates, transitions)
    ]
    return pl.pallas_call(
        functools.partial(inner_kernel, steps, rows),
        out_shape=[
            pltpu.VMEM((steps, rows - 1, columns, bins), F32),
            jax.ShapeDtypeStruct(((rows - 1) * columns + 16, bins), BF16),
            pltpu.VMEM((steps, columns, bins), F32),
            pltpu.VMEM((columns, bins), F32),
            pltpu.VMEM((rows, columns, bins), F32),
            pltpu.VMEM((steps, 2 * bins, 2 * bins), BF16),
        ],
        in_specs=[anywhere, vmem, anywhere, anywhere, anywhere],
        out_specs=[vmem] * 6,
        scratch_shapes=[
            pltpu.VMEM((steps, rows, columns, bins), BF16),
            pltpu.VMEM((rows, columns, bins), F32),
            pltpu.VMEM((steps, bins, bins), F32),
            pltpu.VMEM((rows + 1, columns + 16, bins), F32),
            pltpu.VMEM((rows + 1, columns + 16, bins), F32),
            pltpu.VMEM((rows, columns, bins), F32),
            pltpu.VMEM((rows - 1, columns, bins), F32),
            pltpu.VMEM((rows, columns), F32),
            pltpu.SemaphoreType.DMA((steps,)),
            pltpu.SemaphoreType.DMA,
            pltpu.SemaphoreType.DMA((steps,)),
            pltpu.SemaphoreType.DMA,
        ],
        compiler_params=pltpu.CompilerParams(vmem_limit_bytes=16 * MIB),
        cost_estimate=pl.CostEstimate(
            flops=8 * steps * rows * columns * bins * bins,
            bytes_accessed=steps * rows * columns * bins * 2,
            transcendentals=0,
        ),
        name="inner_rows",
    )(previous, halo, initial, rates, transitions)


def outer_kernel(
    steps, halo_ref, part_ref, first_ref, keep_ref, rhs_ref, most_ref, loc_ref, code_ref, all_ref, state, sem
):
    columns = first_ref.shape[0]
    joined = most_ref.shape[0]
    copy = pltpu.make_async_copy(most_ref, all_ref.at[pl.ds(0, joined)], sem)
    copy.start()
    state[...] = first_ref[...]

    def left_of(t, i, _):
        cells = slice(i * CHUNK, (i + 1) * CHUNK)
        inflow = part_ref[t, cells] + halo_ref[t, cells].astype(F32)
        return left(keep_ref[0, cells] * state[cells] + inflow)

    def store(t, i, both):
        cells = slice(i * CHUNK, (i + 1) * CHUNK)
        state[cells] = loc_ref[t, 0, cells] = halves(both)

    stream(steps, columns // CHUNK, lambda t: rhs_ref[t], left_of, store)
    finish(loc_ref, code_ref, steps)
    all_ref[joined:] = code_ref[...]
    copy.wait()


def outer_row(halo, part, first, keep, rhs, most):
    steps, columns, bins = part.shape
    vmem = pl.BlockSpec(memory_space=pltpu.VMEM)
    return pl.pallas_call(
        functools.partial(outer_kernel, steps),
        out_shape=[
            pltpu.VMEM((steps, 1, columns, bins), F32),
            jax.ShapeDtypeStruct((columns + 16, bins), BF16),
            jax.ShapeDtypeStruct((most.shape[0] + columns + 16, bins), BF16),
        ],
        in_specs=[vmem] * 6,
        out_specs=[vmem] * 3,
        scratch_shapes=[pltpu.VMEM((columns, bins), F32), pltpu.SemaphoreType.DMA],
        compiler_params=pltpu.CompilerParams(vmem_limit_bytes=4 * MIB),
        cost_estimate=pl.CostEstimate(
            flops=0, bytes_accessed=0, transcendentals=0
        ),
        name="outer_row",
    )(halo, part, first, keep, rhs, most)


def product_kernel(steps, trans_ref, prefix_ref, total_ref, work, sems):
    block = lax.axis_index("tm")
    copies = []
    for back in range(3):
        at = pl.ds(jnp.maximum(block - back, 0) * steps, steps)
        copies.append(
            pltpu.make_async_copy(
                trans_ref.at[at], work.at[pl.ds(back * steps, steps)], sems.at[back]
            )
        )
        copies[-1].start()
    for copy in copies:
        copy.wait()
    span = 1
    while span < steps:
        pairs = [(i // span * span - 1, i) for i in range(steps) if i & span]
        for back in (1, 2):
            pairs += [(k, k + span) for k in range(back * steps, (back + 1) * steps, 2 * span)]
        for first, second in pairs:
            product = times(work[first], right(work[second]))
            work[second if second < steps else first] = product
        span *= 2
    for t in range(steps):
        prefix_ref[t] = right(work[t])
    total_ref[0] = right(work[steps])
    total_ref[1] = right(work[2 * steps])


def products(transitions, steps):
    bins = transitions.shape[1]
    transitions = pltpu.with_memory_space_constraint(transitions, pltpu.HBM)
    vmem = pl.BlockSpec(memory_space=pltpu.VMEM)
    return pl.pallas_call(
        functools.partial(product_kernel, steps),
        out_shape=[
            pltpu.VMEM((steps, 2 * bins, 2 * bins), BF16),
            pltpu.VMEM((2, 2 * bins, 2 * bins), BF16),
        ],
        in_specs=[pl.BlockSpec(memory_space=pl.ANY)],
        out_specs=[vmem, vmem],
        scratch_shapes=[
            pltpu.VMEM((3 * steps, bins, bins), F32),
            pltpu.SemaphoreType.DMA((3,)),
        ],
        compiler_params=pltpu.CompilerParams(vmem_limit_bytes=16 * MIB),
        cost_estimate=pl.CostEstimate(
            flops=0, bytes_accessed=0, transcendentals=0
        ),
        name="products",
    )(transitions)


def scale_of(ref, last):
    return ref[last : last + 16].astype(F32)[0:1, 0:1]


def decay(held):
    for _ in range(4):
        held = held * held
    return held


def ready_kernel(calc, near_code, far_code, keep_ref, total_ref, near_ref, far_ref):
    columns = keep_ref.shape[1]
    pieces = [(n, q, c) for n, q in enumerate(calc) for c in range(0, columns, CHUNK)]
    last = len(calc) * columns
    near_scale, far_scale = scale_of(near_code, last), scale_of(far_code, last)

    def left_far(_, i, slot):
        n, _, c = pieces[i]
        return left(decode(far_code[n * columns + c : n * columns + c + CHUNK], far_scale))

    def store(_, i, both):
        n, q, c = pieces[i]
        cells = slice(c, c + CHUNK)
        at = n * columns + c
        near_ref[n, cells] = decode(near_code[at : at + CHUNK], near_scale)
        far_ref[n, cells] = decay(keep_ref[q, cells]) * halves(both)

    stream(1, len(pieces), lambda _: total_ref[1], left_far, store)


def ready(calc, near, far, keep, total):
    _, columns, bins = keep.shape
    vmem = pl.BlockSpec(memory_space=pltpu.VMEM)
    return pl.pallas_call(
        functools.partial(ready_kernel, calc),
        out_shape=[pltpu.VMEM((len(calc), columns, bins), F32)] * 2,
        in_specs=[vmem] * 4,
        out_specs=[vmem] * 2,
        compiler_params=pltpu.CompilerParams(vmem_limit_bytes=4 * MIB),
        cost_estimate=pl.CostEstimate(
            flops=4_000_000_000, bytes_accessed=8_000_000, transcendentals=0
        ),
        name="ready",
    )(near, far, keep, total)


def spread_kernel(
    chunks, rows,
    near1_ref, far1_ref, near0_code, far0_code, mid_ref, loc1_ref, loc0_ref, keep_ref, prefix_ref, total_ref,
    out_ref,
    entering, power, near0_ref, far0_ref, stage, sems,
):
    odd = lax.rem(lax.axis_index("space"), 2)
    steps, _, columns, bins = stage.shape
    locs = (loc1_ref, loc0_ref)
    pieces, at, scales = [], 0, []
    for k, calc in enumerate(chunks):
        for n, q in enumerate(calc):
            pieces += [(k, n, q, c, at + c) for c in range(0, columns, CHUNK)]
            at += columns
        scales.append(scale_of(mid_ref, at))
        at += 16
    count = len(pieces)
    nears, fars = (near1_ref, near0_ref), (far1_ref, far0_ref)
    ready_kernel(chunks[1], near0_code, far0_code, keep_ref, total_ref, near0_ref, far0_ref)

    def cells_of(i):
        return pieces[i][2], slice(pieces[i][3], pieces[i][3] + CHUNK)

    def left_mid(_, i, slot):
        k, n, q, c, at = pieces[i]
        return left(decode(mid_ref[at : at + CHUNK], scales[k]) + fars[k][n, c : c + CHUNK])

    def store_mid(_, i, both):
        k, n, _, c, _ = pieces[i]
        state = nears[k][n, c : c + CHUNK] + decay(keep_ref[cells_of(i)]) * halves(both)
        entering[cells_of(i)] = left(state)
        power[cells_of(i)] = jnp.ones((CHUNK, bins), F32)

    stream(1, count, lambda _: total_ref[0], left_mid, store_mid)

    def store(t, i, both):
        k, n, q, c, _ = pieces[i]
        factor = power[cells_of(i)] * keep_ref[cells_of(i)]
        power[cells_of(i)] = factor
        value = locs[k][t, n, c : c + CHUNK] + factor * halves(both)
        stage[t, place(q, rows, odd), c : c + CHUNK] = value.astype(BF16)
        if i == count - 1:
            pltpu.make_async_copy(stage.at[t], out_ref.at[t], sems.at[t]).start()

    stream(steps, count, lambda t: prefix_ref[t], lambda t, i, slot: entering[cells_of(i)], store)
    for t in range(steps):
        pltpu.make_async_copy(stage.at[t], out_ref.at[t], sems.at[t]).wait()


def spread(chunks, near1, far1, near0, far0, mid, loc1, loc0, keep, prefix, total):
    steps, _, columns, bins = loc1.shape
    rows = keep.shape[0]
    vmem = pl.BlockSpec(memory_space=pltpu.VMEM)
    return pl.pallas_call(
        functools.partial(spread_kernel, chunks, rows),
        out_shape=jax.ShapeDtypeStruct((steps, rows, columns, bins), BF16),
        in_specs=[vmem] * 10,
        out_specs=pl.BlockSpec(memory_space=pl.ANY),
        scratch_shapes=[
            pltpu.VMEM((rows, columns, 2 * bins), BF16),
            pltpu.VMEM((rows, columns, bins), F32),
            pltpu.VMEM((1, columns, bins), F32),
            pltpu.VMEM((1, columns, bins), F32),
            pltpu.VMEM((steps, rows, columns, bins), BF16),
            pltpu.SemaphoreType.DMA((steps,)),
        ],
        compiler_params=pltpu.CompilerParams(vmem_limit_bytes=16 * MIB),
        cost_estimate=pl.CostEstimate(
            flops=8 * steps * rows * columns * bins * bins,
            bytes_accessed=steps * rows * columns * bins * 2,
            transcendentals=0,
        ),
        name="spread",
    )(near1, far1, near0, far0, mid, loc1, loc0, keep, prefix, total)


def local(previous, initial, rates, transitions):
    steps, rows, columns, bins = previous.shape
    strips, blocks = lax.axis_size("space"), lax.axis_size("tm")
    outer_edge, inner_edge = edges(previous, rates)
    between = [(i, i + 1) for i in range(1, strips - 1, 2)]
    within = [(i, i + 1) for i in range(0, strips, 2)]
    outer = lax.ppermute(outer_edge, "space", between + [(j, i) for i, j in between])
    inner = lax.ppermute(inner_edge, "space", within + [(j, i) for i, j in within])

    def send(code, hop):
        return lax.ppermute(code, "tm", [(i, i + hop) for i in range(blocks - hop)])

    most, rest = tuple(range(1, rows)), (0,)
    loc1, code1, part, first, keep, rhs = inner_rows(previous, inner, initial, rates, transitions)
    near1, far1 = send(code1, 1), send(code1, 3)
    loc0, code0, code = outer_row(outer, part, first, keep, rhs, code1)
    mid, near0, far0 = send(code, 2), send(code0, 1), send(code0, 3)
    prefix, total = products(transitions, steps)
    chunks = (most, rest)
    ready1 = ready(most, near1, far1, keep, total)
    return spread(chunks, *ready1, near0, far0, mid, loc1, loc0, keep, prefix, total)


def solution(mesh):
    in_specs = (P("tm", "space", None, None), P("space", None, None), P("space", None), P())
    out_specs = P("tm", "space", None, None)
    return jax.shard_map(local, mesh=mesh, in_specs=in_specs, out_specs=out_specs, check_vma=False)
```

```python
import functools

import jax
import jax.numpy as jnp
from jax import lax
from jax.experimental import pallas as pl
from jax.experimental.pallas import tpu as pltpu
from jax.sharding import PartitionSpec as P

F32, BF16 = jnp.float32, jnp.bfloat16
PEAK = 2.0**15.5
CHUNK = 64
MIB = 1 << 20


def split(value):
    high = value.astype(BF16)
    low = (value - high.astype(F32)).astype(BF16)
    return high, low


def left(value):
    return jnp.concatenate(split(value), axis=1)


def right(matrix):
    both = jnp.concatenate(split(matrix), axis=1)
    return jnp.concatenate([both, both], axis=0)


def times(value, matrix):
    n = matrix.shape[1] // 2
    both = jnp.dot(left(value), matrix, preferred_element_type=F32)
    return both[:, :n] + both[:, n:]


def shares(rates_ref, which, bins):
    lines = [rates_ref[pl.ds(row, 1), :] for row in which]
    lines += [jnp.zeros_like(lines[0])] * (8 - len(lines))
    turned = jnp.concatenate(lines, axis=0).T
    return [jnp.broadcast_to(turned[:, i : i + 1], (turned.shape[0], bins)) for i in range(len(which))]


def place(q, rows, odd):
    return q + odd * (rows - 1 - 2 * q)


def encode(value, scale):
    u = value * (PEAK / scale)
    g = u * u
    g = g * g
    g = g * g
    return jnp.where(value < 0, -g, g).astype(BF16)


def decode(code, scale):
    g = code.astype(F32)
    root = jnp.exp(jnp.log(jnp.abs(g)) * 0.125) * (scale * (1.0 / PEAK))
    return jnp.where(g < 0, -root, root)


def stream(steps, count, matrix_of, left_of, store, beside=None):
    lag = max(n for n in range(2, 13, 2) if count % n == 0)

    def push(t):
        matrix = matrix_of(t)
        pltpu.matmul_push_rhs(matrix, 0, 0)
        pltpu.matmul_push_rhs(matrix, 0, 1)

    def run(*accs):
        def emit(t, first, last, slot):
            for i in range(count):
                acc = accs[i % lag]
                if i >= lag:
                    store(t, i - lag, pltpu.matmul_pop(acc))
                elif not first:
                    store(t - 1, count - lag + i, pltpu.matmul_pop(acc))
                pltpu.matmul_acc_lhs(acc, left_of(t, i, slot), load_staged_rhs=0 if i < 2 else None)
                if i == count // 2 and not last:
                    push(t + 1)
                if beside is not None:
                    beside(t, i, slot)

        push(0)
        emit(0, True, steps == 1, 0)

        def pair(k, carry):
            emit(2 * k + 1, False, False, 1)
            emit(2 * k + 2, False, False, 0)
            return carry

        pairs = max(steps - 2, 0) // 2
        lax.fori_loop(0, pairs, pair, 0)
        for t in range(2 * pairs + 1, steps):
            emit(t, False, t == steps - 1, t % 2)
        for i in range(lag):
            store(steps - 1, count - lag + i, pltpu.matmul_pop(accs[i]))

    pl.run_scoped(run, *[pltpu.ACC(i % 2)((CHUNK, 256), F32) for i in range(lag)])


def halves(both):
    n = both.shape[1] // 2
    return both[:, :n] + both[:, n:]


def finish(loc_ref, code_ref, steps):
    rows, columns, bins = loc_ref.shape[1:]
    top = jnp.zeros((columns, bins), F32)
    for n in range(rows):
        top = jnp.maximum(top, jnp.abs(loc_ref[steps - 1, n]))
    scale = (jnp.max(top, keepdims=True) * 1.01 + 1e-30).astype(BF16).astype(F32)
    for n in range(rows):
        code_ref[n * columns : (n + 1) * columns] = encode(loc_ref[steps - 1, n], scale)
    code_ref[rows * columns :] = jnp.broadcast_to(scale, (16, bins)).astype(BF16)


def edge_kernel(steps, rows, prev_ref, line_ref, outer_ref, inner_ref, buf, rates_ref, sems, rsem):
    odd = lax.rem(lax.axis_index("space"), 2)
    bins = buf.shape[3]
    order = [place(0, rows, odd), place(rows - 1, rows, odd)]
    group = steps // sems.shape[1]

    def fetch(side, k):
        at = pl.ds(k * group, group)
        return pltpu.make_async_copy(
            prev_ref.at[at, order[side]], buf.at[side, at], sems.at[side, k]
        )

    parts = [(side, k) for side in range(2) for k in range(sems.shape[1])]
    lines = pltpu.make_async_copy(line_ref, rates_ref, rsem)
    lines.start()
    for part in parts:
        fetch(*part).start()
    lines.wait()
    weights = [share * 0.25 for share in shares(rates_ref, order, bins)]
    for side, k in parts:
        fetch(side, k).wait()
        out_ref = (outer_ref, inner_ref)[side]
        for t in range(k * group, (k + 1) * group):
            out_ref[t] = (buf[side, t].astype(F32) * weights[side]).astype(BF16)


def edges(previous, rates):
    steps, rows, columns, bins = previous.shape
    vmem = pl.BlockSpec(memory_space=pltpu.VMEM)
    return pl.pallas_call(
        functools.partial(edge_kernel, steps, rows),
        out_shape=[jax.ShapeDtypeStruct((steps, columns, bins), BF16)] * 2,
        in_specs=[pl.BlockSpec(memory_space=pl.ANY)] * 2,
        out_specs=[vmem] * 2,
        scratch_shapes=[
            pltpu.VMEM((2, steps, columns, bins), BF16),
            pltpu.VMEM((rows, columns), F32),
            pltpu.SemaphoreType.DMA((2, 4)),
            pltpu.SemaphoreType.DMA,
        ],
        compiler_params=pltpu.CompilerParams(vmem_limit_bytes=8 * MIB),
        cost_estimate=pl.CostEstimate(flops=0, bytes_accessed=0, transcendentals=0),
        name="edges",
    )(*[pltpu.with_memory_space_constraint(a, pltpu.HBM) for a in (previous, rates)])


def inner_kernel(
    steps, rows,
    prev_ref, halo_ref, init_ref, line_ref, trans_ref,
    loc_ref, code_ref, part_ref, first_ref, keep_ref, rhs_ref,
    pbuf, ibuf, tbuf, even, odds, weight, state, rates_ref, psem, isem, tsem, rsem,
):
    odd = lax.rem(lax.axis_index("space"), 2)
    block = lax.axis_index("tm")
    columns, bins = pbuf.shape[2], pbuf.shape[3]

    def fetch(t):
        return pltpu.make_async_copy(prev_ref.at[t], pbuf.at[t], psem.at[t])

    def matrix(t):
        return pltpu.make_async_copy(trans_ref.at[block * steps + t], tbuf.at[t], tsem.at[t])

    start = pltpu.make_async_copy(init_ref, ibuf, isem)
    lines = pltpu.make_async_copy(line_ref, rates_ref, rsem)
    lines.start()
    matrix(0).start()
    fetch(0).start()
    start.start()
    lines.wait()
    for q, share in enumerate(shares(rates_ref, [place(q, rows, odd) for q in range(rows)], bins)):
        weight[q] = share * 0.25
        keep_ref[q] = 1.0 - share
    grids = (even, odds)
    for grid in grids:
        for i in range(rows + 1):
            grid[i, 0:8] = jnp.zeros((8, bins), F32)
            grid[i, columns + 8 :] = jnp.zeros((8, bins), F32)
    for t in range(1, steps):
        matrix(t).start()
        fetch(t).start()
    matrix(0).wait()
    rhs_ref[0] = right(tbuf[0])
    start.wait()
    for q in range(rows):
        value = ibuf[place(q, rows, odd)]
        value = jnp.where(block == 0, value, jnp.zeros_like(value))
        if q == 0:
            first_ref[...] = value
        else:
            state[q - 1] = value

    pieces = [(q, c) for q in range(1, rows) for c in range(0, columns, CHUNK)]

    units = [(q, c) for q in range(rows + 1) for c in range(0, columns, CHUNK)]

    def fill(t, unit, slot):
        q, c = unit
        if q == rows:
            value = halo_ref[t, c : c + CHUNK].astype(F32)
        else:
            value = pbuf[t, place(q, rows, odd), c : c + CHUNK].astype(F32)
            value = (value * weight[q, c : c + CHUNK]).astype(BF16).astype(F32)
        grids[slot][q, 8 + c : 8 + c + CHUNK] = value

    def sides(grid, q, c):
        return grid[q, 7 + c : 7 + c + CHUNK] + grid[q, 9 + c : 9 + c + CHUNK]

    def left_of(t, i, slot):
        q, c = pieces[i]
        grid, inside, cells = grids[slot], slice(8 + c, 8 + c + CHUNK), slice(c, c + CHUNK)
        inflow = (grid[q - 1, inside] + grid[q + 1, inside]) + sides(grid, q, c)
        return left(keep_ref[q, cells] * state[q - 1, cells] + inflow)

    def store(t, i, both):
        q, c = pieces[i]
        value = halves(both)
        state[q - 1, c : c + CHUNK] = value
        loc_ref[t, q - 1, c : c + CHUNK] = value

    def beside(t, i, slot):
        if i % rows == 0 and i // rows < columns // CHUNK:
            c = i // rows * CHUNK
            grid = grids[slot]
            part_ref[t, c : c + CHUNK] = grid[1, 8 + c : 8 + c + CHUNK] + sides(grid, 0, c)
        if isinstance(t, int) and t == steps - 1:
            return
        if i == 0:
            fetch(t + 1).wait()
        if i == 2:
            matrix(t + 1).wait()
            rhs_ref[t + 1] = right(tbuf[t + 1])
        for unit in units[len(units) * i // len(pieces) : len(units) * (i + 1) // len(pieces)]:
            fill(t + 1, unit, 1 - slot)

    fetch(0).wait()
    for unit in units:
        fill(0, unit, 0)
    stream(steps, len(pieces), lambda t: rhs_ref[t], left_of, store, beside)
    finish(loc_ref, code_ref, steps)


def inner_rows(previous, halo, initial, rates, transitions):
    steps, rows, columns, bins = previous.shape
    anywhere = pl.BlockSpec(memory_space=pl.ANY)
    vmem = pl.BlockSpec(memory_space=pltpu.VMEM)
    previous, initial, rates, transitions = [
        pltpu.with_memory_space_constraint(a, pltpu.HBM)
        for a in (previous, initial, rates, transitions)
    ]
    return pl.pallas_call(
        functools.partial(inner_kernel, steps, rows),
        out_shape=[
            pltpu.VMEM((steps, rows - 1, columns, bins), F32),
            jax.ShapeDtypeStruct(((rows - 1) * columns + 16, bins), BF16),
            pltpu.VMEM((steps, columns, bins), F32),
            pltpu.VMEM((columns, bins), F32),
            pltpu.VMEM((rows, columns, bins), F32),
            pltpu.VMEM((steps, 2 * bins, 2 * bins), BF16),
        ],
        in_specs=[anywhere, vmem, anywhere, anywhere, anywhere],
        out_specs=[vmem] * 6,
        scratch_shapes=[
            pltpu.VMEM((steps, rows, columns, bins), BF16),
            pltpu.VMEM((rows, columns, bins), F32),
            pltpu.VMEM((steps, bins, bins), F32),
            pltpu.VMEM((rows + 1, columns + 16, bins), F32),
            pltpu.VMEM((rows + 1, columns + 16, bins), F32),
            pltpu.VMEM((rows, columns, bins), F32),
            pltpu.VMEM((rows - 1, columns, bins), F32),
            pltpu.VMEM((rows, columns), F32),
            pltpu.SemaphoreType.DMA((steps,)),
            pltpu.SemaphoreType.DMA,
            pltpu.SemaphoreType.DMA((steps,)),
            pltpu.SemaphoreType.DMA,
        ],
        compiler_params=pltpu.CompilerParams(vmem_limit_bytes=16 * MIB),
        cost_estimate=pl.CostEstimate(
            flops=8 * steps * rows * columns * bins * bins,
            bytes_accessed=steps * rows * columns * bins * 2,
            transcendentals=0,
        ),
        name="inner_rows",
    )(previous, halo, initial, rates, transitions)


def outer_kernel(
    steps, halo_ref, part_ref, first_ref, keep_ref, rhs_ref, most_ref, loc_ref, code_ref, all_ref, state, sem
):
    columns = first_ref.shape[0]
    joined = most_ref.shape[0]
    copy = pltpu.make_async_copy(most_ref, all_ref.at[pl.ds(0, joined)], sem)
    copy.start()
    state[...] = first_ref[...]

    def left_of(t, i, _):
        cells = slice(i * CHUNK, (i + 1) * CHUNK)
        inflow = part_ref[t, cells] + halo_ref[t, cells].astype(F32)
        return left(keep_ref[0, cells] * state[cells] + inflow)

    def store(t, i, both):
        cells = slice(i * CHUNK, (i + 1) * CHUNK)
        state[cells] = loc_ref[t, 0, cells] = halves(both)

    stream(steps, columns // CHUNK, lambda t: rhs_ref[t], left_of, store)
    finish(loc_ref, code_ref, steps)
    all_ref[joined:] = code_ref[...]
    copy.wait()


def outer_row(halo, part, first, keep, rhs, most):
    steps, columns, bins = part.shape
    vmem = pl.BlockSpec(memory_space=pltpu.VMEM)
    return pl.pallas_call(
        functools.partial(outer_kernel, steps),
        out_shape=[
            pltpu.VMEM((steps, 1, columns, bins), F32),
            jax.ShapeDtypeStruct((columns + 16, bins), BF16),
            jax.ShapeDtypeStruct((most.shape[0] + columns + 16, bins), BF16),
        ],
        in_specs=[vmem] * 6,
        out_specs=[vmem] * 3,
        scratch_shapes=[pltpu.VMEM((columns, bins), F32), pltpu.SemaphoreType.DMA],
        compiler_params=pltpu.CompilerParams(vmem_limit_bytes=4 * MIB),
        cost_estimate=pl.CostEstimate(
            flops=0, bytes_accessed=0, transcendentals=0
        ),
        name="outer_row",
    )(halo, part, first, keep, rhs, most)


def product_kernel(steps, trans_ref, prefix_ref, total_ref, work, sems):
    block = lax.axis_index("tm")
    copies = []
    for back in range(3):
        at = pl.ds(jnp.maximum(block - back, 0) * steps, steps)
        copies.append(
            pltpu.make_async_copy(
                trans_ref.at[at], work.at[pl.ds(back * steps, steps)], sems.at[back]
            )
        )
        copies[-1].start()
    for copy in copies:
        copy.wait()
    span = 1
    while span < steps:
        pairs = [(i // span * span - 1, i) for i in range(steps) if i & span]
        for back in (1, 2):
            pairs += [(k, k + span) for k in range(back * steps, (back + 1) * steps, 2 * span)]
        for first, second in pairs:
            product = times(work[first], right(work[second]))
            work[second if second < steps else first] = product
        span *= 2
    for t in range(steps):
        prefix_ref[t] = right(work[t])
    total_ref[0] = right(work[steps])
    total_ref[1] = right(work[2 * steps])


def products(transitions, steps):
    bins = transitions.shape[1]
    transitions = pltpu.with_memory_space_constraint(transitions, pltpu.HBM)
    vmem = pl.BlockSpec(memory_space=pltpu.VMEM)
    return pl.pallas_call(
        functools.partial(product_kernel, steps),
        out_shape=[
            pltpu.VMEM((steps, 2 * bins, 2 * bins), BF16),
            pltpu.VMEM((2, 2 * bins, 2 * bins), BF16),
        ],
        in_specs=[pl.BlockSpec(memory_space=pl.ANY)],
        out_specs=[vmem, vmem],
        scratch_shapes=[
            pltpu.VMEM((3 * steps, bins, bins), F32),
            pltpu.SemaphoreType.DMA((3,)),
        ],
        compiler_params=pltpu.CompilerParams(vmem_limit_bytes=16 * MIB),
        cost_estimate=pl.CostEstimate(
            flops=0, bytes_accessed=0, transcendentals=0
        ),
        name="products",
    )(transitions)


def scale_of(ref, last):
    return ref[last : last + 16].astype(F32)[0:1, 0:1]


def decay(held):
    for _ in range(4):
        held = held * held
    return held


def ready_kernel(calc, near_code, far_code, keep_ref, total_ref, near_ref, far_ref):
    columns = keep_ref.shape[1]
    pieces = [(n, q, c) for n, q in enumerate(calc) for c in range(0, columns, CHUNK)]
    last = len(calc) * columns
    near_scale, far_scale = scale_of(near_code, last), scale_of(far_code, last)

    def left_far(_, i, slot):
        n, _, c = pieces[i]
        return left(decode(far_code[n * columns + c : n * columns + c + CHUNK], far_scale))

    def store(_, i, both):
        n, q, c = pieces[i]
        cells = slice(c, c + CHUNK)
        at = n * columns + c
        near_ref[n, cells] = decode(near_code[at : at + CHUNK], near_scale)
        far_ref[n, cells] = decay(keep_ref[q, cells]) * halves(both)

    stream(1, len(pieces), lambda _: total_ref[1], left_far, store)


def chunks_kernel(
    chunks, near1_code, far1_code, near0_code, far0_code, keep_ref, total_ref,
    near1_ref, far1_ref, near0_ref, far0_ref,
):
    ready_kernel(chunks[0], near1_code, far1_code, keep_ref, total_ref, near1_ref, far1_ref)
    ready_kernel(chunks[1], near0_code, far0_code, keep_ref, total_ref, near0_ref, far0_ref)


def ready(chunks, codes, keep, total):
    _, columns, bins = keep.shape
    vmem = pl.BlockSpec(memory_space=pltpu.VMEM)
    return pl.pallas_call(
        functools.partial(chunks_kernel, chunks),
        out_shape=[pltpu.VMEM((len(calc), columns, bins), F32) for calc in chunks for _ in range(2)],
        in_specs=[vmem] * 6,
        out_specs=[vmem] * 4,
        compiler_params=pltpu.CompilerParams(vmem_limit_bytes=4 * MIB),
        cost_estimate=pl.CostEstimate(
            flops=2000000000, bytes_accessed=4000000, transcendentals=0
        ),
        name="ready",
    )(*codes, keep, total)


def spread_kernel(
    chunks, rows,
    near1_ref, far1_ref, near0_ref, far0_ref, mid_ref, loc1_ref, loc0_ref, keep_ref, prefix_ref, total_ref,
    out_ref,
    entering, power, stage, sems,
):
    odd = lax.rem(lax.axis_index("space"), 2)
    steps, _, columns, bins = stage.shape
    locs = (loc1_ref, loc0_ref)
    pieces, at, scales = [], 0, []
    for k, calc in enumerate(chunks):
        for n, q in enumerate(calc):
            pieces += [(k, n, q, c, at + c) for c in range(0, columns, CHUNK)]
            at += columns
        scales.append(scale_of(mid_ref, at))
        at += 16
    count = len(pieces)
    nears, fars = (near1_ref, near0_ref), (far1_ref, far0_ref)

    def cells_of(i):
        return pieces[i][2], slice(pieces[i][3], pieces[i][3] + CHUNK)

    def left_mid(_, i, slot):
        k, n, q, c, at = pieces[i]
        return left(decode(mid_ref[at : at + CHUNK], scales[k]) + fars[k][n, c : c + CHUNK])

    def store_mid(_, i, both):
        k, n, _, c, _ = pieces[i]
        state = nears[k][n, c : c + CHUNK] + decay(keep_ref[cells_of(i)]) * halves(both)
        entering[cells_of(i)] = left(state)
        power[cells_of(i)] = jnp.ones((CHUNK, bins), F32)

    stream(1, count, lambda _: total_ref[0], left_mid, store_mid)

    def store(t, i, both):
        k, n, q, c, _ = pieces[i]
        factor = power[cells_of(i)] * keep_ref[cells_of(i)]
        power[cells_of(i)] = factor
        value = locs[k][t, n, c : c + CHUNK] + factor * halves(both)
        stage[t, place(q, rows, odd), c : c + CHUNK] = value.astype(BF16)
        if i == count - 1:
            pltpu.make_async_copy(stage.at[t], out_ref.at[t], sems.at[t]).start()

    stream(steps, count, lambda t: prefix_ref[t], lambda t, i, slot: entering[cells_of(i)], store)
    for t in range(steps):
        pltpu.make_async_copy(stage.at[t], out_ref.at[t], sems.at[t]).wait()


def spread(chunks, near1, far1, near0, far0, mid, loc1, loc0, keep, prefix, total):
    steps, _, columns, bins = loc1.shape
    rows = keep.shape[0]
    vmem = pl.BlockSpec(memory_space=pltpu.VMEM)
    return pl.pallas_call(
        functools.partial(spread_kernel, chunks, rows),
        out_shape=jax.ShapeDtypeStruct((steps, rows, columns, bins), BF16),
        in_specs=[vmem] * 10,
        out_specs=pl.BlockSpec(memory_space=pl.ANY),
        scratch_shapes=[
            pltpu.VMEM((rows, columns, 2 * bins), BF16),
            pltpu.VMEM((rows, columns, bins), F32),
            pltpu.VMEM((steps, rows, columns, bins), BF16),
            pltpu.SemaphoreType.DMA((steps,)),
        ],
        compiler_params=pltpu.CompilerParams(vmem_limit_bytes=16 * MIB),
        cost_estimate=pl.CostEstimate(
            flops=8 * steps * rows * columns * bins * bins,
            bytes_accessed=steps * rows * columns * bins * 2,
            transcendentals=0,
        ),
        name="spread",
    )(near1, far1, near0, far0, mid, loc1, loc0, keep, prefix, total)


def local(previous, initial, rates, transitions):
    steps, rows, columns, bins = previous.shape
    strips, blocks = lax.axis_size("space"), lax.axis_size("tm")
    outer_edge, inner_edge = edges(previous, rates)
    between = [(i, i + 1) for i in range(1, strips - 1, 2)]
    within = [(i, i + 1) for i in range(0, strips, 2)]
    outer = lax.ppermute(outer_edge, "space", between + [(j, i) for i, j in between])
    inner = lax.ppermute(inner_edge, "space", within + [(j, i) for i, j in within])

    def send(code, hop):
        return lax.ppermute(code, "tm", [(i, i + hop) for i in range(blocks - hop)])

    chunks = most, rest = tuple(range(1, rows)), (0,)
    loc1, code1, part, first, keep, rhs = inner_rows(previous, inner, initial, rates, transitions)
    near1, far1 = send(code1, 1), send(code1, 3)
    loc0, code0, code = outer_row(outer, part, first, keep, rhs, code1)
    mid, near0, far0 = send(code, 2), send(code0, 1), send(code0, 3)
    prefix, total = products(transitions, steps)
    chunks = (most, rest)
    brought = ready(chunks, [near1, far1, near0, far0], keep, total)
    return spread(chunks, *brought, mid, loc1, loc0, keep, prefix, total)


def solution(mesh):
    in_specs = (P("tm", "space", None, None), P("space", None, None), P("space", None), P())
    out_specs = P("tm", "space", None, None)
    return jax.shard_map(local, mesh=mesh, in_specs=in_specs, out_specs=out_specs, check_vma=False)
```

```python
import functools

import jax
import jax.numpy as jnp
from jax import lax
from jax.experimental import pallas as pl
from jax.experimental.pallas import tpu as pltpu
from jax.sharding import PartitionSpec as P

F32, BF16 = jnp.float32, jnp.bfloat16
PEAK = 2.0**15.5
CHUNK = 64
MIB = 1 << 20


def split(value):
    high = value.astype(BF16)
    low = (value - high.astype(F32)).astype(BF16)
    return high, low


def left(value):
    return jnp.concatenate(split(value), axis=1)


def right(matrix):
    both = jnp.concatenate(split(matrix), axis=1)
    return jnp.concatenate([both, both], axis=0)


def times(value, matrix):
    n = matrix.shape[1] // 2
    both = jnp.dot(left(value), matrix, preferred_element_type=F32)
    return both[:, :n] + both[:, n:]


def shares(rates_ref, which, bins):
    lines = [rates_ref[pl.ds(row, 1), :] for row in which]
    lines += [jnp.zeros_like(lines[0])] * (8 - len(lines))
    turned = jnp.concatenate(lines, axis=0).T
    return [jnp.broadcast_to(turned[:, i : i + 1], (turned.shape[0], bins)) for i in range(len(which))]


def place(q, rows, odd):
    return q + odd * (rows - 1 - 2 * q)


def encode(value, scale):
    u = value * (PEAK / scale)
    g = u * u
    g = g * g
    g = g * g
    return jnp.where(value < 0, -g, g).astype(BF16)


def decode(code, scale):
    g = code.astype(F32)
    root = jnp.exp(jnp.log(jnp.abs(g)) * 0.125) * (scale * (1.0 / PEAK))
    return jnp.where(g < 0, -root, root)


def stream(steps, count, matrix_of, left_of, store, beside=None):
    lag = max(n for n in range(2, 13, 2) if count % n == 0)

    def push(t):
        matrix = matrix_of(t)
        pltpu.matmul_push_rhs(matrix, 0, 0)
        pltpu.matmul_push_rhs(matrix, 0, 1)

    def run(*accs):
        def emit(t, first, last, slot):
            for i in range(count):
                acc = accs[i % lag]
                if i >= lag:
                    store(t, i - lag, pltpu.matmul_pop(acc))
                elif not first:
                    store(t - 1, count - lag + i, pltpu.matmul_pop(acc))
                pltpu.matmul_acc_lhs(acc, left_of(t, i, slot), load_staged_rhs=0 if i < 2 else None)
                if i == count // 2 and not last:
                    push(t + 1)
                if beside is not None:
                    beside(t, i, slot)

        push(0)
        emit(0, True, steps == 1, 0)

        def pair(k, carry):
            emit(2 * k + 1, False, False, 1)
            emit(2 * k + 2, False, False, 0)
            return carry

        pairs = max(steps - 2, 0) // 2
        lax.fori_loop(0, pairs, pair, 0)
        for t in range(2 * pairs + 1, steps):
            emit(t, False, t == steps - 1, t % 2)
        for i in range(lag):
            store(steps - 1, count - lag + i, pltpu.matmul_pop(accs[i]))

    pl.run_scoped(run, *[pltpu.ACC(i % 2)((CHUNK, 256), F32) for i in range(lag)])


def halves(both):
    n = both.shape[1] // 2
    return both[:, :n] + both[:, n:]


def finish(loc_ref, code_ref, steps):
    rows, columns, bins = loc_ref.shape[1:]
    top = jnp.zeros((columns, bins), F32)
    for n in range(rows):
        top = jnp.maximum(top, jnp.abs(loc_ref[steps - 1, n]))
    scale = (jnp.max(top, keepdims=True) * 1.01 + 1e-30).astype(BF16).astype(F32)
    for n in range(rows):
        code_ref[n * columns : (n + 1) * columns] = encode(loc_ref[steps - 1, n], scale)
    code_ref[rows * columns :] = jnp.broadcast_to(scale, (16, bins)).astype(BF16)


def edge_kernel(steps, rows, prev_ref, line_ref, outer_ref, inner_ref, buf, rates_ref, sems, rsem):
    odd = lax.rem(lax.axis_index("space"), 2)
    bins = buf.shape[3]
    order = [place(0, rows, odd), place(rows - 1, rows, odd)]
    group = steps // sems.shape[1]

    def fetch(side, k):
        at = pl.ds(k * group, group)
        return pltpu.make_async_copy(
            prev_ref.at[at, order[side]], buf.at[side, at], sems.at[side, k]
        )

    parts = [(side, k) for side in range(2) for k in range(sems.shape[1])]
    lines = pltpu.make_async_copy(line_ref, rates_ref, rsem)
    lines.start()
    for part in parts:
        fetch(*part).start()
    lines.wait()
    weights = [share * 0.25 for share in shares(rates_ref, order, bins)]
    for side, k in parts:
        fetch(side, k).wait()
        out_ref = (outer_ref, inner_ref)[side]
        for t in range(k * group, (k + 1) * group):
            out_ref[t] = (buf[side, t].astype(F32) * weights[side]).astype(BF16)


def edges(previous, rates):
    steps, rows, columns, bins = previous.shape
    vmem = pl.BlockSpec(memory_space=pltpu.VMEM)
    return pl.pallas_call(
        functools.partial(edge_kernel, steps, rows),
        out_shape=[jax.ShapeDtypeStruct((steps, columns, bins), BF16)] * 2,
        in_specs=[pl.BlockSpec(memory_space=pl.ANY)] * 2,
        out_specs=[vmem] * 2,
        scratch_shapes=[
            pltpu.VMEM((2, steps, columns, bins), BF16),
            pltpu.VMEM((rows, columns), F32),
            pltpu.SemaphoreType.DMA((2, 4)),
            pltpu.SemaphoreType.DMA,
        ],
        compiler_params=pltpu.CompilerParams(vmem_limit_bytes=8 * MIB),
        cost_estimate=pl.CostEstimate(flops=0, bytes_accessed=0, transcendentals=0),
        name="edges",
    )(*[pltpu.with_memory_space_constraint(a, pltpu.HBM) for a in (previous, rates)])


def inner_kernel(
    steps, rows,
    prev_ref, halo_ref, init_ref, line_ref, trans_ref,
    loc_ref, code_ref, tail_ref, part_ref, first_ref, keep_ref, rhs_ref,
    pbuf, ibuf, tbuf, even, odds, weight, state, rates_ref, psem, isem, tsem, rsem,
):
    odd = lax.rem(lax.axis_index("space"), 2)
    block = lax.axis_index("tm")
    columns, bins = pbuf.shape[2], pbuf.shape[3]

    def fetch(t):
        return pltpu.make_async_copy(prev_ref.at[t], pbuf.at[t], psem.at[t])

    def matrix(t):
        return pltpu.make_async_copy(trans_ref.at[block * steps + t], tbuf.at[t], tsem.at[t])

    start = pltpu.make_async_copy(init_ref, ibuf, isem)
    lines = pltpu.make_async_copy(line_ref, rates_ref, rsem)
    lines.start()
    matrix(0).start()
    fetch(0).start()
    start.start()
    lines.wait()
    for q, share in enumerate(shares(rates_ref, [place(q, rows, odd) for q in range(rows)], bins)):
        weight[q] = share * 0.25
        keep_ref[q] = 1.0 - share
    grids = (even, odds)
    for grid in grids:
        for i in range(rows + 1):
            grid[i, 0:8] = jnp.zeros((8, bins), F32)
            grid[i, columns + 8 :] = jnp.zeros((8, bins), F32)
    for t in range(1, steps):
        matrix(t).start()
        fetch(t).start()
    matrix(0).wait()
    rhs_ref[0] = right(tbuf[0])
    start.wait()
    for q in range(rows):
        value = ibuf[place(q, rows, odd)]
        value = jnp.where(block == 0, value, jnp.zeros_like(value))
        if q == 0:
            first_ref[...] = value
        else:
            state[q - 1] = value

    pieces = [(q, c) for q in range(1, rows) for c in range(0, columns, CHUNK)]

    units = [(q, c) for q in range(rows + 1) for c in range(0, columns, CHUNK)]

    def fill(t, unit, slot):
        q, c = unit
        if q == rows:
            value = halo_ref[t, c : c + CHUNK].astype(F32)
        else:
            value = pbuf[t, place(q, rows, odd), c : c + CHUNK].astype(F32)
            value = (value * weight[q, c : c + CHUNK]).astype(BF16).astype(F32)
        grids[slot][q, 8 + c : 8 + c + CHUNK] = value

    def sides(grid, q, c):
        return grid[q, 7 + c : 7 + c + CHUNK] + grid[q, 9 + c : 9 + c + CHUNK]

    def left_of(t, i, slot):
        q, c = pieces[i]
        grid, inside, cells = grids[slot], slice(8 + c, 8 + c + CHUNK), slice(c, c + CHUNK)
        inflow = (grid[q - 1, inside] + grid[q + 1, inside]) + sides(grid, q, c)
        return left(keep_ref[q, cells] * state[q - 1, cells] + inflow)

    def store(t, i, both):
        q, c = pieces[i]
        value = halves(both)
        state[q - 1, c : c + CHUNK] = value
        loc_ref[t, q - 1, c : c + CHUNK] = value

    def beside(t, i, slot):
        if i % rows == 0 and i // rows < columns // CHUNK:
            c = i // rows * CHUNK
            grid = grids[slot]
            part_ref[t, c : c + CHUNK] = grid[1, 8 + c : 8 + c + CHUNK] + sides(grid, 0, c)
        if isinstance(t, int) and t == steps - 1:
            return
        if i == 0:
            fetch(t + 1).wait()
        if i == 2:
            matrix(t + 1).wait()
            rhs_ref[t + 1] = right(tbuf[t + 1])
        for unit in units[len(units) * i // len(pieces) : len(units) * (i + 1) // len(pieces)]:
            fill(t + 1, unit, 1 - slot)

    fetch(0).wait()
    for unit in units:
        fill(0, unit, 0)
    stream(steps, len(pieces), lambda t: rhs_ref[t], left_of, store, beside)
    finish(loc_ref, code_ref, steps)
    tail_ref[...] = code_ref[code_ref.shape[0] - tail_ref.shape[0] :]


def inner_rows(previous, halo, initial, rates, transitions):
    steps, rows, columns, bins = previous.shape
    anywhere = pl.BlockSpec(memory_space=pl.ANY)
    vmem = pl.BlockSpec(memory_space=pltpu.VMEM)
    previous, initial, rates, transitions = [
        pltpu.with_memory_space_constraint(a, pltpu.HBM)
        for a in (previous, initial, rates, transitions)
    ]
    return pl.pallas_call(
        functools.partial(inner_kernel, steps, rows),
        out_shape=[
            pltpu.VMEM((steps, rows - 1, columns, bins), F32),
            jax.ShapeDtypeStruct(((rows - 1) * columns + 16, bins), BF16),
            jax.ShapeDtypeStruct((rows // 2 * columns + 16, bins), BF16),
            pltpu.VMEM((steps, columns, bins), F32),
            pltpu.VMEM((columns, bins), F32),
            pltpu.VMEM((rows, columns, bins), F32),
            pltpu.VMEM((steps, 2 * bins, 2 * bins), BF16),
        ],
        in_specs=[anywhere, vmem, anywhere, anywhere, anywhere],
        out_specs=[vmem] * 7,
        scratch_shapes=[
            pltpu.VMEM((steps, rows, columns, bins), BF16),
            pltpu.VMEM((rows, columns, bins), F32),
            pltpu.VMEM((steps, bins, bins), F32),
            pltpu.VMEM((rows + 1, columns + 16, bins), F32),
            pltpu.VMEM((rows + 1, columns + 16, bins), F32),
            pltpu.VMEM((rows, columns, bins), F32),
            pltpu.VMEM((rows - 1, columns, bins), F32),
            pltpu.VMEM((rows, columns), F32),
            pltpu.SemaphoreType.DMA((steps,)),
            pltpu.SemaphoreType.DMA,
            pltpu.SemaphoreType.DMA((steps,)),
            pltpu.SemaphoreType.DMA,
        ],
        compiler_params=pltpu.CompilerParams(vmem_limit_bytes=16 * MIB),
        cost_estimate=pl.CostEstimate(
            flops=8 * steps * rows * columns * bins * bins,
            bytes_accessed=steps * rows * columns * bins * 2,
            transcendentals=0,
        ),
        name="inner_rows",
    )(previous, halo, initial, rates, transitions)


def outer_kernel(
    steps, halo_ref, part_ref, first_ref, keep_ref, rhs_ref, most_ref, after_ref, loc_ref, code_ref, all_ref, state, sem
):
    columns = first_ref.shape[0]
    joined = all_ref.shape[0] - code_ref.shape[0]
    copy = pltpu.make_async_copy(
        most_ref.at[pl.ds(0, joined - 16)], all_ref.at[pl.ds(0, joined - 16)], sem
    )
    copy.start()
    state[...] = first_ref[...]

    def left_of(t, i, _):
        cells = slice(i * CHUNK, (i + 1) * CHUNK)
        inflow = part_ref[t, cells] + halo_ref[t, cells].astype(F32)
        return left(keep_ref[0, cells] * state[cells] + inflow)

    def store(t, i, both):
        cells = slice(i * CHUNK, (i + 1) * CHUNK)
        state[cells] = loc_ref[t, 0, cells] = halves(both)

    stream(steps, columns // CHUNK, lambda t: rhs_ref[t], left_of, store)
    finish(loc_ref, code_ref, steps)
    all_ref[joined - 16 : joined] = most_ref[most_ref.shape[0] - 16 :]
    all_ref[joined:] = code_ref[...]
    copy.wait()


def outer_row(halo, part, first, keep, rhs, most, after):
    steps, columns, bins = part.shape
    rows = keep.shape[0]
    vmem = pl.BlockSpec(memory_space=pltpu.VMEM)
    return pl.pallas_call(
        functools.partial(outer_kernel, steps),
        out_shape=[
            pltpu.VMEM((steps, 1, columns, bins), F32),
            jax.ShapeDtypeStruct((columns + 16, bins), BF16),
            jax.ShapeDtypeStruct(((rows - rows // 2) * columns + 32, bins), BF16),
        ],
        in_specs=[vmem] * 6 + [pl.BlockSpec(memory_space=pl.ANY)],
        out_specs=[vmem] * 3,
        scratch_shapes=[pltpu.VMEM((columns, bins), F32), pltpu.SemaphoreType.DMA],
        compiler_params=pltpu.CompilerParams(vmem_limit_bytes=4 * MIB),
        cost_estimate=pl.CostEstimate(
            flops=0, bytes_accessed=0, transcendentals=0
        ),
        name="outer_row",
    )(halo, part, first, keep, rhs, most, after)


def product_kernel(steps, trans_ref, prefix_ref, total_ref, work, sems):
    block = lax.axis_index("tm")
    copies = []
    for back in range(3):
        at = pl.ds(jnp.maximum(block - back, 0) * steps, steps)
        copies.append(
            pltpu.make_async_copy(
                trans_ref.at[at], work.at[pl.ds(back * steps, steps)], sems.at[back]
            )
        )
        copies[-1].start()
    for copy in copies:
        copy.wait()
    span = 1
    while span < steps:
        pairs = [(i // span * span - 1, i) for i in range(steps) if i & span]
        for back in (1, 2):
            pairs += [(k, k + span) for k in range(back * steps, (back + 1) * steps, 2 * span)]
        for first, second in pairs:
            product = times(work[first], right(work[second]))
            work[second if second < steps else first] = product
        span *= 2
    for t in range(steps):
        prefix_ref[t] = right(work[t])
    total_ref[0] = right(work[steps])
    total_ref[1] = right(work[2 * steps])


def products(transitions, steps):
    bins = transitions.shape[1]
    transitions = pltpu.with_memory_space_constraint(transitions, pltpu.HBM)
    vmem = pl.BlockSpec(memory_space=pltpu.VMEM)
    return pl.pallas_call(
        functools.partial(product_kernel, steps),
        out_shape=[
            pltpu.VMEM((steps, 2 * bins, 2 * bins), BF16),
            pltpu.VMEM((2, 2 * bins, 2 * bins), BF16),
        ],
        in_specs=[pl.BlockSpec(memory_space=pl.ANY)],
        out_specs=[vmem, vmem],
        scratch_shapes=[
            pltpu.VMEM((3 * steps, bins, bins), F32),
            pltpu.SemaphoreType.DMA((3,)),
        ],
        compiler_params=pltpu.CompilerParams(vmem_limit_bytes=16 * MIB),
        cost_estimate=pl.CostEstimate(
            flops=1000000000, bytes_accessed=0, transcendentals=0
        ),
        name="products",
    )(transitions)


def scale_of(ref, last):
    return ref[last : last + 16].astype(F32)[0:1, 0:1]


def decay(held):
    for _ in range(4):
        held = held * held
    return held


def ready_kernel(calc, near_code, far_code, keep_ref, total_ref, near_ref, far_ref):
    columns = keep_ref.shape[1]
    pieces = [(n, q, c) for n, q in enumerate(calc) for c in range(0, columns, CHUNK)]
    last = len(calc) * columns
    near_scale, far_scale = scale_of(near_code, last), scale_of(far_code, last)

    def left_far(_, i, slot):
        n, _, c = pieces[i]
        return left(decode(far_code[n * columns + c : n * columns + c + CHUNK], far_scale))

    def store(_, i, both):
        n, q, c = pieces[i]
        cells = slice(c, c + CHUNK)
        at = n * columns + c
        near_ref[n, cells] = decode(near_code[at : at + CHUNK], near_scale)
        far_ref[n, cells] = decay(keep_ref[q, cells]) * halves(both)

    stream(1, len(pieces), lambda _: total_ref[1], left_far, store)


def ready(calc, near, far, keep, total):
    _, columns, bins = keep.shape
    vmem = pl.BlockSpec(memory_space=pltpu.VMEM)
    return pl.pallas_call(
        functools.partial(ready_kernel, calc),
        out_shape=[pltpu.VMEM((len(calc), columns, bins), F32)] * 2,
        in_specs=[vmem] * 4,
        out_specs=[vmem] * 2,
        compiler_params=pltpu.CompilerParams(vmem_limit_bytes=4 * MIB),
        cost_estimate=pl.CostEstimate(
            flops=1000000000, bytes_accessed=2000000, transcendentals=0
        ),
        name="ready",
    )(near, far, keep, total)


def spread_kernel(chunks, rows, *refs):
    sources, refs = len(chunks), list(refs)
    nears, fars, locs = [[refs.pop(0) for _ in chunks] for _ in range(3)]
    mid_ref, keep_ref, prefix_ref, total_ref = [refs.pop(0) for _ in range(4)]
    *_, out_ref, entering, power, near0_ref, far0_ref, stage, sems = refs
    odd = lax.rem(lax.axis_index("space"), 2)
    steps, held, columns, bins = stage.shape
    picked = [q for calc in chunks for _, q in calc]
    base = jnp.minimum(place(min(picked), rows, odd), place(max(picked), rows, odd))
    pieces, at, scales = [], 0, []
    for k, calc in enumerate(chunks):
        for n, q in calc:
            pieces += [(k, n, q, c, at + c) for c in range(0, columns, CHUNK)]
            at += columns
        scales.append(scale_of(mid_ref, at))
        at += 16
    count = len(pieces)
    if sources > 1:
        ready_kernel((0,), nears[1], fars[1], keep_ref, total_ref, near0_ref, far0_ref)
        nears[1], fars[1] = near0_ref, far0_ref

    def copy(t):
        return pltpu.make_async_copy(stage.at[t], out_ref.at[t, pl.ds(base, held)], sems.at[t])

    def cells_of(i):
        return pieces[i][2], slice(pieces[i][3], pieces[i][3] + CHUNK)

    def left_mid(_, i, slot):
        k, n, q, c, at = pieces[i]
        return left(decode(mid_ref[at : at + CHUNK], scales[k]) + fars[k][n, c : c + CHUNK])

    def store_mid(_, i, both):
        k, n, _, c, _ = pieces[i]
        state = nears[k][n, c : c + CHUNK] + decay(keep_ref[cells_of(i)]) * halves(both)
        entering[pieces[i][2], cells_of(i)[1]] = left(state)
        power[cells_of(i)] = jnp.ones((CHUNK, bins), F32)

    stream(1, count, lambda _: total_ref[0], left_mid, store_mid)

    def store(t, i, both):
        k, n, q, c, _ = pieces[i]
        factor = power[cells_of(i)] * keep_ref[cells_of(i)]
        power[cells_of(i)] = factor
        value = locs[k][t, n, c : c + CHUNK] + factor * halves(both)
        stage[t, place(q, rows, odd) - base, c : c + CHUNK] = value.astype(BF16)
        if i == count - 1:
            copy(t).start()

    stream(steps, count, lambda t: prefix_ref[t], lambda t, i, slot: entering[cells_of(i)], store)
    for t in range(steps):
        copy(t).wait()


def spread(chunks, nears, fars, locs, mid, keep, prefix, total, before=None):
    steps, _, columns, bins = locs[0].shape
    rows = keep.shape[0]
    held = sum(len(calc) for calc in chunks)
    vmem, anywhere = pl.BlockSpec(memory_space=pltpu.VMEM), pl.BlockSpec(memory_space=pl.ANY)
    arrays = [*nears, *fars, *locs, mid, keep, prefix, total]
    specs = [vmem] * len(arrays)
    aliases = {}
    if before is not None:
        aliases = {len(arrays): 0}
        arrays, specs = arrays + [before], specs + [anywhere]
    return pl.pallas_call(
        functools.partial(spread_kernel, chunks, rows),
        out_shape=jax.ShapeDtypeStruct((steps, rows, columns, bins), BF16),
        in_specs=specs,
        out_specs=anywhere,
        scratch_shapes=[
            pltpu.VMEM((rows, columns, 2 * bins), BF16),
            pltpu.VMEM((rows, columns, bins), F32),
            pltpu.VMEM((1, columns, bins), F32),
            pltpu.VMEM((1, columns, bins), F32),
            pltpu.VMEM((steps, held, columns, bins), BF16),
            pltpu.SemaphoreType.DMA((steps,)),
        ],
        input_output_aliases=aliases,
        compiler_params=pltpu.CompilerParams(vmem_limit_bytes=16 * MIB),
        cost_estimate=pl.CostEstimate(
            flops=1000000000, bytes_accessed=2000000,
            transcendentals=0,
        ),
        name=f"spread{len(chunks)}",
    )(*arrays)


def local(previous, initial, rates, transitions):
    steps, rows, columns, bins = previous.shape
    strips, blocks = lax.axis_size("space"), lax.axis_size("tm")
    outer_edge, inner_edge = edges(previous, rates)
    between = [(i, i + 1) for i in range(1, strips - 1, 2)]
    within = [(i, i + 1) for i in range(0, strips, 2)]
    outer = lax.ppermute(outer_edge, "space", between + [(j, i) for i, j in between])
    inner = lax.ppermute(inner_edge, "space", within + [(j, i) for i, j in within])

    def send(code, hop):
        return lax.ppermute(code, "tm", [(i, i + hop) for i in range(blocks - hop)])

    most, half = tuple(range(1, rows)), rows - rows // 2
    loc1, code1, tail, part, first, keep, rhs = inner_rows(
        previous, inner, initial, rates, transitions
    )
    near1, far1, mid1 = send(code1, 1), send(code1, 3), send(tail, 2)
    prefix, total = products(transitions, steps)
    loc0, code0, code = outer_row(outer, part, first, keep, rhs, code1, total)
    mid0, near0, far0 = send(code, 2), send(code0, 1), send(code0, 3)
    near1, far1 = ready(most, near1, far1, keep, total)
    later = (tuple((q - 1, q) for q in range(half, rows)),)
    early = (tuple((q - 1, q) for q in range(1, half)), ((0, 0),))
    out = spread(later, [near1], [far1], [loc1], mid1, keep, prefix, total)
    return spread(
        early, [near1, near0], [far1, far0], [loc1, loc0], mid0, keep, prefix, total, out
    )


def solution(mesh):
    in_specs = (P("tm", "space", None, None), P("space", None, None), P("space", None), P())
    out_specs = P("tm", "space", None, None)
    return jax.shard_map(local, mesh=mesh, in_specs=in_specs, out_specs=out_specs, check_vma=False)
```

```python
import functools

import jax
import jax.numpy as jnp
from jax import lax
from jax.experimental import pallas as pl
from jax.experimental.pallas import tpu as pltpu
from jax.sharding import PartitionSpec as P

F32, BF16 = jnp.float32, jnp.bfloat16
PEAK = 2.0**15.5
CHUNK = 64
MIB = 1 << 20


def split(value):
    high = value.astype(BF16)
    low = (value - high.astype(F32)).astype(BF16)
    return high, low


def left(value):
    return jnp.concatenate(split(value), axis=1)


def right(matrix):
    both = jnp.concatenate(split(matrix), axis=1)
    return jnp.concatenate([both, both], axis=0)


def times(value, matrix):
    n = matrix.shape[1] // 2
    both = jnp.dot(left(value), matrix, preferred_element_type=F32)
    return both[:, :n] + both[:, n:]


def shares(rates_ref, which, bins):
    lines = [rates_ref[pl.ds(row, 1), :] for row in which]
    lines += [jnp.zeros_like(lines[0])] * (8 - len(lines))
    turned = jnp.concatenate(lines, axis=0).T
    return [jnp.broadcast_to(turned[:, i : i + 1], (turned.shape[0], bins)) for i in range(len(which))]


def place(q, rows, odd):
    return q + odd * (rows - 1 - 2 * q)


def encode(value, scale):
    u = value * (PEAK / scale)
    g = u * u
    g = g * g
    g = g * g
    return jnp.where(value < 0, -g, g).astype(BF16)


def decode(code, scale):
    g = code.astype(F32)
    root = jnp.exp(jnp.log(jnp.abs(g)) * 0.125) * (scale * (1.0 / PEAK))
    return jnp.where(g < 0, -root, root)


def stream(steps, count, matrix_of, left_of, store, beside=None):
    lag = max(n for n in range(2, 13, 2) if count % n == 0)

    def push(t):
        matrix = matrix_of(t)
        pltpu.matmul_push_rhs(matrix, 0, 0)
        pltpu.matmul_push_rhs(matrix, 0, 1)

    def run(*accs):
        def emit(t, first, last, slot):
            for i in range(count):
                acc = accs[i % lag]
                if i >= lag:
                    store(t, i - lag, pltpu.matmul_pop(acc))
                elif not first:
                    store(t - 1, count - lag + i, pltpu.matmul_pop(acc))
                pltpu.matmul_acc_lhs(acc, left_of(t, i, slot), load_staged_rhs=0 if i < 2 else None)
                if i == count // 2 and not last:
                    push(t + 1)
                if beside is not None:
                    beside(t, i, slot)

        push(0)
        emit(0, True, steps == 1, 0)

        def pair(k, carry):
            emit(2 * k + 1, False, False, 1)
            emit(2 * k + 2, False, False, 0)
            return carry

        pairs = max(steps - 2, 0) // 2
        lax.fori_loop(0, pairs, pair, 0)
        for t in range(2 * pairs + 1, steps):
            emit(t, False, t == steps - 1, t % 2)
        for i in range(lag):
            store(steps - 1, count - lag + i, pltpu.matmul_pop(accs[i]))

    pl.run_scoped(run, *[pltpu.ACC(i % 2)((CHUNK, 256), F32) for i in range(lag)])


def halves(both):
    n = both.shape[1] // 2
    return both[:, :n] + both[:, n:]


def finish(loc_ref, code_ref, steps):
    rows, columns, bins = loc_ref.shape[1:]
    top = jnp.zeros((columns, bins), F32)
    for n in range(rows):
        top = jnp.maximum(top, jnp.abs(loc_ref[steps - 1, n]))
    scale = (jnp.max(top, keepdims=True) * 1.01 + 1e-30).astype(BF16).astype(F32)
    for n in range(rows):
        code_ref[n * columns : (n + 1) * columns] = encode(loc_ref[steps - 1, n], scale)
    code_ref[rows * columns :] = jnp.broadcast_to(scale, (16, bins)).astype(BF16)


def edge_kernel(steps, rows, prev_ref, line_ref, outer_ref, inner_ref, buf, rates_ref, sems, rsem):
    odd = lax.rem(lax.axis_index("space"), 2)
    bins = buf.shape[3]
    order = [place(0, rows, odd), place(rows - 1, rows, odd)]
    group = steps // sems.shape[1]

    def fetch(side, k):
        at = pl.ds(k * group, group)
        return pltpu.make_async_copy(
            prev_ref.at[at, order[side]], buf.at[side, at], sems.at[side, k]
        )

    parts = [(side, k) for side in range(2) for k in range(sems.shape[1])]
    lines = pltpu.make_async_copy(line_ref, rates_ref, rsem)
    lines.start()
    for part in parts:
        fetch(*part).start()
    lines.wait()
    weights = [share * 0.25 for share in shares(rates_ref, order, bins)]
    for side, k in parts:
        fetch(side, k).wait()
        out_ref = (outer_ref, inner_ref)[side]
        for t in range(k * group, (k + 1) * group):
            out_ref[t] = (buf[side, t].astype(F32) * weights[side]).astype(BF16)


def edges(previous, rates):
    steps, rows, columns, bins = previous.shape
    vmem = pl.BlockSpec(memory_space=pltpu.VMEM)
    return pl.pallas_call(
        functools.partial(edge_kernel, steps, rows),
        out_shape=[jax.ShapeDtypeStruct((steps, columns, bins), BF16)] * 2,
        in_specs=[pl.BlockSpec(memory_space=pl.ANY)] * 2,
        out_specs=[vmem] * 2,
        scratch_shapes=[
            pltpu.VMEM((2, steps, columns, bins), BF16),
            pltpu.VMEM((rows, columns), F32),
            pltpu.SemaphoreType.DMA((2, 4)),
            pltpu.SemaphoreType.DMA,
        ],
        compiler_params=pltpu.CompilerParams(vmem_limit_bytes=8 * MIB),
        cost_estimate=pl.CostEstimate(flops=0, bytes_accessed=0, transcendentals=0),
        name="edges",
    )(*[pltpu.with_memory_space_constraint(a, pltpu.HBM) for a in (previous, rates)])


def inner_kernel(
    steps, rows,
    prev_ref, init_ref, line_ref, trans_ref,
    loc_ref, code_ref, part_ref, first_ref, keep_ref, rhs_ref,
    pbuf, ibuf, tbuf, even, odds, weight, state, rates_ref, psem, isem, tsem, rsem,
):
    odd = lax.rem(lax.axis_index("space"), 2)
    block = lax.axis_index("tm")
    columns, bins = pbuf.shape[2], pbuf.shape[3]

    def fetch(t):
        return pltpu.make_async_copy(prev_ref.at[t], pbuf.at[t], psem.at[t])

    def matrix(t):
        return pltpu.make_async_copy(trans_ref.at[block * steps + t], tbuf.at[t], tsem.at[t])

    start = pltpu.make_async_copy(init_ref, ibuf, isem)
    lines = pltpu.make_async_copy(line_ref, rates_ref, rsem)
    lines.start()
    matrix(0).start()
    fetch(0).start()
    start.start()
    lines.wait()
    for q, share in enumerate(shares(rates_ref, [place(q, rows, odd) for q in range(rows)], bins)):
        weight[q] = share * 0.25
        keep_ref[q] = 1.0 - share
    grids = (even, odds)
    for grid in grids:
        for i in range(rows):
            grid[i, 0:8] = jnp.zeros((8, bins), F32)
            grid[i, columns + 8 :] = jnp.zeros((8, bins), F32)
    for t in range(1, steps):
        matrix(t).start()
        fetch(t).start()
    matrix(0).wait()
    rhs_ref[0] = right(tbuf[0])
    start.wait()
    for q in range(rows):
        value = ibuf[place(q, rows, odd)]
        value = jnp.where(block == 0, value, jnp.zeros_like(value))
        if q in (0, rows - 1):
            first_ref[min(q, 1)] = value
        else:
            state[q - 1] = value

    pieces = [(q, c) for q in range(1, rows - 1) for c in range(0, columns, CHUNK)]

    units = [(q, c) for q in range(rows) for c in range(0, columns, CHUNK)]

    def fill(t, unit, slot):
        q, c = unit
        value = pbuf[t, place(q, rows, odd), c : c + CHUNK].astype(F32)
        value = (value * weight[q, c : c + CHUNK]).astype(BF16).astype(F32)
        grids[slot][q, 8 + c : 8 + c + CHUNK] = value

    def sides(grid, q, c):
        return grid[q, 7 + c : 7 + c + CHUNK] + grid[q, 9 + c : 9 + c + CHUNK]

    def left_of(t, i, slot):
        q, c = pieces[i]
        grid, inside, cells = grids[slot], slice(8 + c, 8 + c + CHUNK), slice(c, c + CHUNK)
        inflow = (grid[q - 1, inside] + grid[q + 1, inside]) + sides(grid, q, c)
        return left(keep_ref[q, cells] * state[q - 1, cells] + inflow)

    def store(t, i, both):
        q, c = pieces[i]
        value = halves(both)
        state[q - 1, c : c + CHUNK] = value
        loc_ref[t, q - 1, c : c + CHUNK] = value

    def beside(t, i, slot):
        every = rows - 2
        if i % every == 0:
            c = i // every * CHUNK
            grid, inside = grids[slot], slice(8 + c, 8 + c + CHUNK)
            part_ref[t, 0, c : c + CHUNK] = grid[1, inside] + sides(grid, 0, c)
            part_ref[t, 1, c : c + CHUNK] = grid[rows - 2, inside] + sides(grid, rows - 1, c)
        if isinstance(t, int) and t == steps - 1:
            return
        if i == 0:
            fetch(t + 1).wait()
        if i == 2:
            matrix(t + 1).wait()
            rhs_ref[t + 1] = right(tbuf[t + 1])
        for unit in units[len(units) * i // len(pieces) : len(units) * (i + 1) // len(pieces)]:
            fill(t + 1, unit, 1 - slot)

    fetch(0).wait()
    for unit in units:
        fill(0, unit, 0)
    stream(steps, len(pieces), lambda t: rhs_ref[t], left_of, store, beside)
    finish(loc_ref, code_ref, steps)


def inner_rows(previous, initial, rates, transitions):
    steps, rows, columns, bins = previous.shape
    anywhere = pl.BlockSpec(memory_space=pl.ANY)
    vmem = pl.BlockSpec(memory_space=pltpu.VMEM)
    previous, initial, rates, transitions = [
        pltpu.with_memory_space_constraint(a, pltpu.HBM)
        for a in (previous, initial, rates, transitions)
    ]
    return pl.pallas_call(
        functools.partial(inner_kernel, steps, rows),
        out_shape=[
            pltpu.VMEM((steps, rows - 2, columns, bins), F32),
            jax.ShapeDtypeStruct(((rows - 2) * columns + 16, bins), BF16),
            pltpu.VMEM((steps, 2, columns, bins), F32),
            pltpu.VMEM((2, columns, bins), F32),
            pltpu.VMEM((rows, columns, bins), F32),
            pltpu.VMEM((steps, 2 * bins, 2 * bins), BF16),
        ],
        in_specs=[anywhere] * 4,
        out_specs=[vmem] * 6,
        scratch_shapes=[
            pltpu.VMEM((steps, rows, columns, bins), BF16),
            pltpu.VMEM((rows, columns, bins), F32),
            pltpu.VMEM((steps, bins, bins), F32),
            pltpu.VMEM((rows, columns + 16, bins), F32),
            pltpu.VMEM((rows, columns + 16, bins), F32),
            pltpu.VMEM((rows, columns, bins), F32),
            pltpu.VMEM((rows - 2, columns, bins), F32),
            pltpu.VMEM((rows, columns), F32),
            pltpu.SemaphoreType.DMA((steps,)),
            pltpu.SemaphoreType.DMA,
            pltpu.SemaphoreType.DMA((steps,)),
            pltpu.SemaphoreType.DMA,
        ],
        compiler_params=pltpu.CompilerParams(vmem_limit_bytes=16 * MIB),
        cost_estimate=pl.CostEstimate(
            flops=8 * steps * rows * columns * bins * bins,
            bytes_accessed=steps * rows * columns * bins * 2,
            transcendentals=0,
        ),
        name="inner_rows",
    )(previous, initial, rates, transitions)


def outer_kernel(
    steps, outer_ref, inner_ref, part_ref, first_ref, keep_ref, rhs_ref, after_ref, loc_ref, code_ref, state
):
    columns = first_ref.shape[1]
    last = keep_ref.shape[0] - 1
    state[...] = first_ref[...]
    pieces = [(k, slice(c, c + CHUNK)) for c in range(0, columns, CHUNK) for k in range(2)]

    def left_of(t, i, _):
        k, cells = pieces[i]
        inflow = part_ref[t, k, cells] + (outer_ref, inner_ref)[k][t, cells].astype(F32)
        return left(keep_ref[k * last, cells] * state[k, cells] + inflow)

    def store(t, i, both):
        state[pieces[i]] = loc_ref[(t, *pieces[i])] = halves(both)

    stream(steps, len(pieces), lambda t: rhs_ref[t], left_of, store)
    finish(loc_ref, code_ref, steps)


def outer_rows(outer, inner, part, first, keep, rhs, after):
    steps, two, columns, bins = part.shape
    vmem = pl.BlockSpec(memory_space=pltpu.VMEM)
    return pl.pallas_call(
        functools.partial(outer_kernel, steps),
        out_shape=[
            pltpu.VMEM((steps, two, columns, bins), F32),
            jax.ShapeDtypeStruct((two * columns + 16, bins), BF16),
        ],
        in_specs=[vmem] * 6 + [pl.BlockSpec(memory_space=pl.ANY)],
        out_specs=[vmem] * 2,
        scratch_shapes=[pltpu.VMEM((two, columns, bins), F32)],
        compiler_params=pltpu.CompilerParams(vmem_limit_bytes=4 * MIB),
        cost_estimate=pl.CostEstimate(
            flops=0, bytes_accessed=0, transcendentals=0
        ),
        name="outer_rows",
    )(outer, inner, part, first, keep, rhs, after)


def product_kernel(steps, trans_ref, prefix_ref, total_ref, work, sems):
    block = lax.axis_index("tm")
    copies = []
    for back in range(3):
        at = pl.ds(jnp.maximum(block - back, 0) * steps, steps)
        copies.append(
            pltpu.make_async_copy(
                trans_ref.at[at], work.at[pl.ds(back * steps, steps)], sems.at[back]
            )
        )
        copies[-1].start()
    for copy in copies:
        copy.wait()
    span = 1
    while span < steps:
        pairs = [(i // span * span - 1, i) for i in range(steps) if i & span]
        for back in (1, 2):
            pairs += [(k, k + span) for k in range(back * steps, (back + 1) * steps, 2 * span)]
        for first, second in pairs:
            product = times(work[first], right(work[second]))
            work[second if second < steps else first] = product
        span *= 2
    for t in range(steps):
        prefix_ref[t] = right(work[t])
    total_ref[0] = right(work[steps])
    total_ref[1] = right(work[2 * steps])


def products(transitions, steps):
    bins = transitions.shape[1]
    transitions = pltpu.with_memory_space_constraint(transitions, pltpu.HBM)
    vmem = pl.BlockSpec(memory_space=pltpu.VMEM)
    return pl.pallas_call(
        functools.partial(product_kernel, steps),
        out_shape=[
            pltpu.VMEM((steps, 2 * bins, 2 * bins), BF16),
            pltpu.VMEM((2, 2 * bins, 2 * bins), BF16),
        ],
        in_specs=[pl.BlockSpec(memory_space=pl.ANY)],
        out_specs=[vmem, vmem],
        scratch_shapes=[
            pltpu.VMEM((3 * steps, bins, bins), F32),
            pltpu.SemaphoreType.DMA((3,)),
        ],
        compiler_params=pltpu.CompilerParams(vmem_limit_bytes=16 * MIB),
        cost_estimate=pl.CostEstimate(
            flops=1000000000, bytes_accessed=0, transcendentals=0
        ),
        name="products",
    )(transitions)


def scale_of(ref, last):
    return ref[last : last + 16].astype(F32)[0:1, 0:1]


def decay(held):
    for _ in range(4):
        held = held * held
    return held


def ready_kernel(calc, near_code, far_code, keep_ref, total_ref, near_ref, far_ref):
    columns = keep_ref.shape[1]
    pieces = [(n, q, c) for n, q in enumerate(calc) for c in range(0, columns, CHUNK)]
    last = len(calc) * columns
    near_scale, far_scale = scale_of(near_code, last), scale_of(far_code, last)

    def left_far(_, i, slot):
        n, _, c = pieces[i]
        return left(decode(far_code[n * columns + c : n * columns + c + CHUNK], far_scale))

    def store(_, i, both):
        n, q, c = pieces[i]
        cells = slice(c, c + CHUNK)
        at = n * columns + c
        near_ref[n, cells] = decode(near_code[at : at + CHUNK], near_scale)
        far_ref[n, cells] = decay(keep_ref[q, cells]) * halves(both)

    stream(1, len(pieces), lambda _: total_ref[1], left_far, store)


def ready(calc, near, far, keep, total):
    _, columns, bins = keep.shape
    vmem = pl.BlockSpec(memory_space=pltpu.VMEM)
    return pl.pallas_call(
        functools.partial(ready_kernel, calc),
        out_shape=[pltpu.VMEM((len(calc), columns, bins), F32)] * 2,
        in_specs=[vmem] * 4,
        out_specs=[vmem] * 2,
        compiler_params=pltpu.CompilerParams(vmem_limit_bytes=4 * MIB),
        cost_estimate=pl.CostEstimate(
            flops=1000000000, bytes_accessed=2000000, transcendentals=0
        ),
        name="ready",
    )(near, far, keep, total)


def spread_kernel(
    chunks, rows,
    near1_ref, far1_ref, near0_code, far0_code, mid1_ref, mid0_ref, loc1_ref, loc0_ref, keep_ref, prefix_ref, total_ref,
    out_ref,
    entering, power, near0_ref, far0_ref, stage, sems,
):
    odd = lax.rem(lax.axis_index("space"), 2)
    steps, _, columns, bins = stage.shape
    locs = (loc1_ref, loc0_ref)
    mids = (mid1_ref, mid0_ref)
    pieces, scales = [], []
    for k, calc in enumerate(chunks):
        for n, q in enumerate(calc):
            pieces += [(k, n, q, c, n * columns + c) for c in range(0, columns, CHUNK)]
        scales.append(scale_of(mids[k], len(calc) * columns))
    count = len(pieces)
    nears, fars = (near1_ref, near0_ref), (far1_ref, far0_ref)
    ready_kernel(chunks[1], near0_code, far0_code, keep_ref, total_ref, near0_ref, far0_ref)

    def cells_of(i):
        return pieces[i][2], slice(pieces[i][3], pieces[i][3] + CHUNK)

    def left_mid(_, i, slot):
        k, n, q, c, at = pieces[i]
        return left(decode(mids[k][at : at + CHUNK], scales[k]) + fars[k][n, c : c + CHUNK])

    def store_mid(_, i, both):
        k, n, _, c, _ = pieces[i]
        state = nears[k][n, c : c + CHUNK] + decay(keep_ref[cells_of(i)]) * halves(both)
        entering[cells_of(i)] = left(state)
        power[cells_of(i)] = jnp.ones((CHUNK, bins), F32)

    stream(1, count, lambda _: total_ref[0], left_mid, store_mid)

    def store(t, i, both):
        k, n, q, c, _ = pieces[i]
        factor = power[cells_of(i)] * keep_ref[cells_of(i)]
        power[cells_of(i)] = factor
        value = locs[k][t, n, c : c + CHUNK] + factor * halves(both)
        stage[t, place(q, rows, odd), c : c + CHUNK] = value.astype(BF16)
        if i == count - 1:
            pltpu.make_async_copy(stage.at[t], out_ref.at[t], sems.at[t]).start()

    stream(steps, count, lambda t: prefix_ref[t], lambda t, i, slot: entering[cells_of(i)], store)
    for t in range(steps):
        pltpu.make_async_copy(stage.at[t], out_ref.at[t], sems.at[t]).wait()


def spread(chunks, near1, far1, near0, far0, mid1, mid0, loc1, loc0, keep, prefix, total):
    steps, _, columns, bins = loc1.shape
    rows = keep.shape[0]
    vmem = pl.BlockSpec(memory_space=pltpu.VMEM)
    return pl.pallas_call(
        functools.partial(spread_kernel, chunks, rows),
        out_shape=jax.ShapeDtypeStruct((steps, rows, columns, bins), BF16),
        in_specs=[vmem] * 11,
        out_specs=pl.BlockSpec(memory_space=pl.ANY),
        scratch_shapes=[
            pltpu.VMEM((rows, columns, 2 * bins), BF16),
            pltpu.VMEM((rows, columns, bins), F32),
            pltpu.VMEM((2, columns, bins), F32),
            pltpu.VMEM((2, columns, bins), F32),
            pltpu.VMEM((steps, rows, columns, bins), BF16),
            pltpu.SemaphoreType.DMA((steps,)),
        ],
        compiler_params=pltpu.CompilerParams(vmem_limit_bytes=16 * MIB),
        cost_estimate=pl.CostEstimate(
            flops=8 * steps * rows * columns * bins * bins,
            bytes_accessed=steps * rows * columns * bins * 2,
            transcendentals=0,
        ),
        name="spread",
    )(near1, far1, near0, far0, mid1, mid0, loc1, loc0, keep, prefix, total)


def local(previous, initial, rates, transitions):
    steps, rows, columns, bins = previous.shape
    strips, blocks = lax.axis_size("space"), lax.axis_size("tm")
    outer_edge, inner_edge = edges(previous, rates)
    between = [(i, i + 1) for i in range(1, strips - 1, 2)]
    within = [(i, i + 1) for i in range(0, strips, 2)]
    outer = lax.ppermute(outer_edge, "space", between + [(j, i) for i, j in between])
    inner = lax.ppermute(inner_edge, "space", within + [(j, i) for i, j in within])

    def send(code, hop):
        return lax.ppermute(code, "tm", [(i, i + hop) for i in range(blocks - hop)])

    most, rest = tuple(range(1, rows - 1)), (0, rows - 1)
    loc1, code1, part, first, keep, rhs = inner_rows(previous, initial, rates, transitions)
    near1, far1, mid1 = send(code1, 1), send(code1, 3), send(code1, 2)
    prefix, total = products(transitions, steps)
    loc0, code0 = outer_rows(outer, inner, part, first, keep, rhs, code1)
    near0, far0, mid0 = send(code0, 1), send(code0, 3), send(code0, 2)
    ready1 = ready(most, near1, far1, keep, total)
    return spread(
        (most, rest), *ready1, near0, far0, mid1, mid0, loc1, loc0, keep, prefix, total
    )


def solution(mesh):
    in_specs = (P("tm", "space", None, None), P("space", None, None), P("space", None), P())
    out_specs = P("tm", "space", None, None)
    return jax.shard_map(local, mesh=mesh, in_specs=in_specs, out_specs=out_specs, check_vma=False)
```

```python
import functools

import jax
import jax.numpy as jnp
from jax import lax
from jax.experimental import pallas as pl
from jax.experimental.pallas import tpu as pltpu
from jax.sharding import PartitionSpec as P

F32, BF16 = jnp.float32, jnp.bfloat16
PEAK = 2.0**15.5
CHUNK = 64
MIB = 1 << 20


def split(value):
    high = value.astype(BF16)
    low = (value - high.astype(F32)).astype(BF16)
    return high, low


def left(value):
    return jnp.concatenate(split(value), axis=1)


def right(matrix):
    both = jnp.concatenate(split(matrix), axis=1)
    return jnp.concatenate([both, both], axis=0)


def times(value, matrix):
    n = matrix.shape[1] // 2
    both = jnp.dot(left(value), matrix, preferred_element_type=F32)
    return both[:, :n] + both[:, n:]


def shares(rates_ref, which, bins):
    lines = [rates_ref[pl.ds(row, 1), :] for row in which]
    lines += [jnp.zeros_like(lines[0])] * (8 - len(lines))
    turned = jnp.concatenate(lines, axis=0).T
    return [jnp.broadcast_to(turned[:, i : i + 1], (turned.shape[0], bins)) for i in range(len(which))]


def place(q, rows, odd):
    return q + odd * (rows - 1 - 2 * q)


def encode(value, scale):
    u = value * (PEAK / scale)
    g = u * u
    g = g * g
    g = g * g
    return jnp.where(value < 0, -g, g).astype(BF16)


def decode(code, scale):
    g = code.astype(F32)
    root = jnp.exp(jnp.log(jnp.abs(g)) * 0.125) * (scale * (1.0 / PEAK))
    return jnp.where(g < 0, -root, root)


def stream(steps, count, matrix_of, left_of, store, beside=None):
    lag = max(n for n in range(2, 13, 2) if count % n == 0)

    def push(t):
        matrix = matrix_of(t)
        pltpu.matmul_push_rhs(matrix, 0, 0)
        pltpu.matmul_push_rhs(matrix, 0, 1)

    def run(*accs):
        def emit(t, first, last, slot):
            for i in range(count):
                acc = accs[i % lag]
                if i >= lag:
                    store(t, i - lag, pltpu.matmul_pop(acc))
                elif not first:
                    store(t - 1, count - lag + i, pltpu.matmul_pop(acc))
                pltpu.matmul_acc_lhs(acc, left_of(t, i, slot), load_staged_rhs=0 if i < 2 else None)
                if i == count // 2 and not last:
                    push(t + 1)
                if beside is not None:
                    beside(t, i, slot)

        push(0)
        emit(0, True, steps == 1, 0)

        def pair(k, carry):
            emit(2 * k + 1, False, False, 1)
            emit(2 * k + 2, False, False, 0)
            return carry

        pairs = max(steps - 2, 0) // 2
        lax.fori_loop(0, pairs, pair, 0)
        for t in range(2 * pairs + 1, steps):
            emit(t, False, t == steps - 1, t % 2)
        for i in range(lag):
            store(steps - 1, count - lag + i, pltpu.matmul_pop(accs[i]))

    pl.run_scoped(run, *[pltpu.ACC(i % 2)((CHUNK, 256), F32) for i in range(lag)])


def halves(both):
    n = both.shape[1] // 2
    return both[:, :n] + both[:, n:]


def finish(loc_ref, code_ref, steps):
    rows, columns, bins = loc_ref.shape[1:]
    top = jnp.zeros((columns, bins), F32)
    for n in range(rows):
        top = jnp.maximum(top, jnp.abs(loc_ref[steps - 1, n]))
    scale = (jnp.max(top, keepdims=True) * 1.01 + 1e-30).astype(BF16).astype(F32)
    for n in range(rows):
        code_ref[n * columns : (n + 1) * columns] = encode(loc_ref[steps - 1, n], scale)
    code_ref[rows * columns :] = jnp.broadcast_to(scale, (16, bins)).astype(BF16)


def edge_kernel(steps, rows, prev_ref, line_ref, outer_ref, inner_ref, buf, rates_ref, sems, rsem):
    odd = lax.rem(lax.axis_index("space"), 2)
    bins = buf.shape[3]
    order = [place(0, rows, odd), place(rows - 1, rows, odd)]
    group = steps // sems.shape[1]

    def fetch(side, k):
        at = pl.ds(k * group, group)
        return pltpu.make_async_copy(
            prev_ref.at[at, order[side]], buf.at[side, at], sems.at[side, k]
        )

    parts = [(side, k) for side in range(2) for k in range(sems.shape[1])]
    lines = pltpu.make_async_copy(line_ref, rates_ref, rsem)
    lines.start()
    for part in parts:
        fetch(*part).start()
    lines.wait()
    weights = [share * 0.25 for share in shares(rates_ref, order, bins)]
    for side, k in parts:
        fetch(side, k).wait()
        out_ref = (outer_ref, inner_ref)[side]
        for t in range(k * group, (k + 1) * group):
            out_ref[t] = (buf[side, t].astype(F32) * weights[side]).astype(BF16)


def edges(previous, rates):
    steps, rows, columns, bins = previous.shape
    vmem = pl.BlockSpec(memory_space=pltpu.VMEM)
    return pl.pallas_call(
        functools.partial(edge_kernel, steps, rows),
        out_shape=[jax.ShapeDtypeStruct((steps, columns, bins), BF16)] * 2,
        in_specs=[pl.BlockSpec(memory_space=pl.ANY)] * 2,
        out_specs=[vmem] * 2,
        scratch_shapes=[
            pltpu.VMEM((2, steps, columns, bins), BF16),
            pltpu.VMEM((rows, columns), F32),
            pltpu.SemaphoreType.DMA((2, 8)),
            pltpu.SemaphoreType.DMA,
        ],
        compiler_params=pltpu.CompilerParams(vmem_limit_bytes=8 * MIB),
        cost_estimate=pl.CostEstimate(flops=0, bytes_accessed=0, transcendentals=0),
        name="edges",
    )(*[pltpu.with_memory_space_constraint(a, pltpu.HBM) for a in (previous, rates)])


def inner_kernel(
    steps, rows,
    prev_ref, halo_ref, init_ref, line_ref, trans_ref,
    loc_ref, code_ref, part_ref, first_ref, keep_ref, rhs_ref,
    pbuf, ibuf, tbuf, even, odds, weight, state, rates_ref, psem, isem, tsem, rsem,
):
    odd = lax.rem(lax.axis_index("space"), 2)
    block = lax.axis_index("tm")
    columns, bins = pbuf.shape[2], pbuf.shape[3]

    def fetch(t):
        return pltpu.make_async_copy(prev_ref.at[t], pbuf.at[t], psem.at[t])

    def matrix(t):
        return pltpu.make_async_copy(trans_ref.at[block * steps + t], tbuf.at[t], tsem.at[t])

    start = pltpu.make_async_copy(init_ref, ibuf, isem)
    lines = pltpu.make_async_copy(line_ref, rates_ref, rsem)
    lines.start()
    matrix(0).start()
    fetch(0).start()
    start.start()
    lines.wait()
    for q, share in enumerate(shares(rates_ref, [place(q, rows, odd) for q in range(rows)], bins)):
        weight[q] = share * 0.25
        keep_ref[q] = 1.0 - share
    grids = (even, odds)
    for grid in grids:
        for i in range(rows + 1):
            grid[i, 0:8] = jnp.zeros((8, bins), F32)
            grid[i, columns + 8 :] = jnp.zeros((8, bins), F32)
    for t in range(1, steps):
        matrix(t).start()
        fetch(t).start()
    matrix(0).wait()
    rhs_ref[0] = right(tbuf[0])
    start.wait()
    for q in range(rows):
        value = ibuf[place(q, rows, odd)]
        value = jnp.where(block == 0, value, jnp.zeros_like(value))
        if q == 0:
            first_ref[...] = value
        else:
            state[q - 1] = value

    pieces = [(q, c) for q in range(1, rows) for c in range(0, columns, CHUNK)]

    units = [(q, c) for q in range(rows + 1) for c in range(0, columns, CHUNK)]

    def fill(t, unit, slot):
        q, c = unit
        if q == rows:
            value = halo_ref[t, c : c + CHUNK].astype(F32)
        else:
            value = pbuf[t, place(q, rows, odd), c : c + CHUNK].astype(F32)
            value = (value * weight[q, c : c + CHUNK]).astype(BF16).astype(F32)
        grids[slot][q, 8 + c : 8 + c + CHUNK] = value

    def sides(grid, q, c):
        return grid[q, 7 + c : 7 + c + CHUNK] + grid[q, 9 + c : 9 + c + CHUNK]

    def left_of(t, i, slot):
        q, c = pieces[i]
        grid, inside, cells = grids[slot], slice(8 + c, 8 + c + CHUNK), slice(c, c + CHUNK)
        inflow = (grid[q - 1, inside] + grid[q + 1, inside]) + sides(grid, q, c)
        return left(keep_ref[q, cells] * state[q - 1, cells] + inflow)

    def store(t, i, both):
        q, c = pieces[i]
        value = halves(both)
        state[q - 1, c : c + CHUNK] = value
        loc_ref[t, q - 1, c : c + CHUNK] = value

    def beside(t, i, slot):
        if i % rows == 0 and i // rows < columns // CHUNK:
            c = i // rows * CHUNK
            grid = grids[slot]
            part_ref[t, c : c + CHUNK] = grid[1, 8 + c : 8 + c + CHUNK] + sides(grid, 0, c)
        if isinstance(t, int) and t == steps - 1:
            return
        if i == 0:
            fetch(t + 1).wait()
        if i == 2:
            matrix(t + 1).wait()
            rhs_ref[t + 1] = right(tbuf[t + 1])
        for unit in units[len(units) * i // len(pieces) : len(units) * (i + 1) // len(pieces)]:
            fill(t + 1, unit, 1 - slot)

    fetch(0).wait()
    for unit in units:
        fill(0, unit, 0)
    stream(steps, len(pieces), lambda t: rhs_ref[t], left_of, store, beside)
    finish(loc_ref, code_ref, steps)


def inner_rows(previous, halo, initial, rates, transitions):
    steps, rows, columns, bins = previous.shape
    anywhere = pl.BlockSpec(memory_space=pl.ANY)
    vmem = pl.BlockSpec(memory_space=pltpu.VMEM)
    previous, initial, rates, transitions = [
        pltpu.with_memory_space_constraint(a, pltpu.HBM)
        for a in (previous, initial, rates, transitions)
    ]
    return pl.pallas_call(
        functools.partial(inner_kernel, steps, rows),
        out_shape=[
            pltpu.VMEM((steps, rows - 1, columns, bins), F32),
            jax.ShapeDtypeStruct(((rows - 1) * columns + 16, bins), BF16),
            pltpu.VMEM((steps, columns, bins), F32),
            pltpu.VMEM((columns, bins), F32),
            pltpu.VMEM((rows, columns, bins), F32),
            pltpu.VMEM((steps, 2 * bins, 2 * bins), BF16),
        ],
        in_specs=[anywhere, vmem, anywhere, anywhere, anywhere],
        out_specs=[vmem] * 6,
        scratch_shapes=[
            pltpu.VMEM((steps, rows, columns, bins), BF16),
            pltpu.VMEM((rows, columns, bins), F32),
            pltpu.VMEM((steps, bins, bins), F32),
            pltpu.VMEM((rows + 1, columns + 16, bins), F32),
            pltpu.VMEM((rows + 1, columns + 16, bins), F32),
            pltpu.VMEM((rows, columns, bins), F32),
            pltpu.VMEM((rows - 1, columns, bins), F32),
            pltpu.VMEM((rows, columns), F32),
            pltpu.SemaphoreType.DMA((steps,)),
            pltpu.SemaphoreType.DMA,
            pltpu.SemaphoreType.DMA((steps,)),
            pltpu.SemaphoreType.DMA,
        ],
        compiler_params=pltpu.CompilerParams(vmem_limit_bytes=16 * MIB),
        cost_estimate=pl.CostEstimate(
            flops=8 * steps * rows * columns * bins * bins,
            bytes_accessed=steps * rows * columns * bins * 2,
            transcendentals=0,
        ),
        name="inner_rows",
    )(previous, halo, initial, rates, transitions)


def outer_kernel(
    steps, halo_ref, part_ref, first_ref, keep_ref, rhs_ref, most_ref, loc_ref, code_ref, all_ref, state, sem
):
    columns = first_ref.shape[0]
    joined = most_ref.shape[0]
    copy = pltpu.make_async_copy(most_ref, all_ref.at[pl.ds(0, joined)], sem)
    copy.start()
    state[...] = first_ref[...]

    def left_of(t, i, _):
        cells = slice(i * CHUNK, (i + 1) * CHUNK)
        inflow = part_ref[t, cells] + halo_ref[t, cells].astype(F32)
        return left(keep_ref[0, cells] * state[cells] + inflow)

    def store(t, i, both):
        cells = slice(i * CHUNK, (i + 1) * CHUNK)
        state[cells] = loc_ref[t, 0, cells] = halves(both)

    stream(steps, columns // CHUNK, lambda t: rhs_ref[t], left_of, store)
    finish(loc_ref, code_ref, steps)
    all_ref[joined:] = code_ref[...]
    copy.wait()


def outer_row(halo, part, first, keep, rhs, most):
    steps, columns, bins = part.shape
    vmem = pl.BlockSpec(memory_space=pltpu.VMEM)
    return pl.pallas_call(
        functools.partial(outer_kernel, steps),
        out_shape=[
            pltpu.VMEM((steps, 1, columns, bins), F32),
            jax.ShapeDtypeStruct((columns + 16, bins), BF16),
            jax.ShapeDtypeStruct((most.shape[0] + columns + 16, bins), BF16),
        ],
        in_specs=[vmem] * 6,
        out_specs=[vmem] * 3,
        scratch_shapes=[pltpu.VMEM((columns, bins), F32), pltpu.SemaphoreType.DMA],
        compiler_params=pltpu.CompilerParams(vmem_limit_bytes=4 * MIB),
        cost_estimate=pl.CostEstimate(
            flops=0, bytes_accessed=0, transcendentals=0
        ),
        name="outer_row",
    )(halo, part, first, keep, rhs, most)


def product_kernel(steps, trans_ref, prefix_ref, total_ref, work, sems):
    block = lax.axis_index("tm")
    copies = []
    for back in range(3):
        at = pl.ds(jnp.maximum(block - back, 0) * steps, steps)
        copies.append(
            pltpu.make_async_copy(
                trans_ref.at[at], work.at[pl.ds(back * steps, steps)], sems.at[back]
            )
        )
        copies[-1].start()
    for copy in copies:
        copy.wait()
    span = 1
    while span < steps:
        pairs = [(i // span * span - 1, i) for i in range(steps) if i & span]
        for back in (1, 2):
            pairs += [(k, k + span) for k in range(back * steps, (back + 1) * steps, 2 * span)]
        for first, second in pairs:
            product = times(work[first], right(work[second]))
            work[second if second < steps else first] = product
        span *= 2
    for t in range(steps):
        prefix_ref[t] = right(work[t])
    total_ref[0] = right(work[steps])
    total_ref[1] = right(work[2 * steps])


def products(transitions, steps):
    bins = transitions.shape[1]
    transitions = pltpu.with_memory_space_constraint(transitions, pltpu.HBM)
    vmem = pl.BlockSpec(memory_space=pltpu.VMEM)
    return pl.pallas_call(
        functools.partial(product_kernel, steps),
        out_shape=[
            pltpu.VMEM((steps, 2 * bins, 2 * bins), BF16),
            pltpu.VMEM((2, 2 * bins, 2 * bins), BF16),
        ],
        in_specs=[pl.BlockSpec(memory_space=pl.ANY)],
        out_specs=[vmem, vmem],
        scratch_shapes=[
            pltpu.VMEM((3 * steps, bins, bins), F32),
            pltpu.SemaphoreType.DMA((3,)),
        ],
        compiler_params=pltpu.CompilerParams(vmem_limit_bytes=16 * MIB),
        cost_estimate=pl.CostEstimate(
            flops=0, bytes_accessed=0, transcendentals=0
        ),
        name="products",
    )(transitions)


def scale_of(ref, last):
    return ref[last : last + 16].astype(F32)[0:1, 0:1]


def decay(held):
    for _ in range(4):
        held = held * held
    return held


def ready_kernel(calc, near_code, far_code, keep_ref, total_ref, near_ref, far_ref):
    columns = keep_ref.shape[1]
    pieces = [(n, q, c) for n, q in enumerate(calc) for c in range(0, columns, CHUNK)]
    last = len(calc) * columns
    near_scale, far_scale = scale_of(near_code, last), scale_of(far_code, last)

    def left_far(_, i, slot):
        n, _, c = pieces[i]
        return left(decode(far_code[n * columns + c : n * columns + c + CHUNK], far_scale))

    def store(_, i, both):
        n, q, c = pieces[i]
        cells = slice(c, c + CHUNK)
        at = n * columns + c
        near_ref[n, cells] = decode(near_code[at : at + CHUNK], near_scale)
        far_ref[n, cells] = decay(keep_ref[q, cells]) * halves(both)

    stream(1, len(pieces), lambda _: total_ref[1], left_far, store)


def ready(calc, near, far, keep, total):
    _, columns, bins = keep.shape
    vmem = pl.BlockSpec(memory_space=pltpu.VMEM)
    return pl.pallas_call(
        functools.partial(ready_kernel, calc),
        out_shape=[pltpu.VMEM((len(calc), columns, bins), F32)] * 2,
        in_specs=[vmem] * 4,
        out_specs=[vmem] * 2,
        compiler_params=pltpu.CompilerParams(vmem_limit_bytes=4 * MIB),
        cost_estimate=pl.CostEstimate(
            flops=4_000_000_000, bytes_accessed=8_000_000, transcendentals=0
        ),
        name="ready",
    )(near, far, keep, total)


def spread_kernel(
    chunks, rows,
    near1_ref, far1_ref, near0_code, far0_code, mid_ref, loc1_ref, loc0_ref, keep_ref, prefix_ref, total_ref,
    out_ref,
    entering, power, near0_ref, far0_ref, stage, sems,
):
    odd = lax.rem(lax.axis_index("space"), 2)
    steps, _, columns, bins = stage.shape
    locs = (loc1_ref, loc0_ref)
    pieces, at, scales = [], 0, []
    for k, calc in enumerate(chunks):
        for n, q in enumerate(calc):
            pieces += [(k, n, q, c, at + c) for c in range(0, columns, CHUNK)]
            at += columns
        scales.append(scale_of(mid_ref, at))
        at += 16
    count = len(pieces)
    nears, fars = (near1_ref, near0_ref), (far1_ref, far0_ref)
    ready_kernel(chunks[1], near0_code, far0_code, keep_ref, total_ref, near0_ref, far0_ref)

    def cells_of(i):
        return pieces[i][2], slice(pieces[i][3], pieces[i][3] + CHUNK)

    def left_mid(_, i, slot):
        k, n, q, c, at = pieces[i]
        return left(decode(mid_ref[at : at + CHUNK], scales[k]) + fars[k][n, c : c + CHUNK])

    def store_mid(_, i, both):
        k, n, _, c, _ = pieces[i]
        state = nears[k][n, c : c + CHUNK] + decay(keep_ref[cells_of(i)]) * halves(both)
        entering[cells_of(i)] = left(state)
        power[cells_of(i)] = jnp.ones((CHUNK, bins), F32)

    stream(1, count, lambda _: total_ref[0], left_mid, store_mid)

    def store(t, i, both):
        k, n, q, c, _ = pieces[i]
        factor = power[cells_of(i)] * keep_ref[cells_of(i)]
        power[cells_of(i)] = factor
        value = locs[k][t, n, c : c + CHUNK] + factor * halves(both)
        stage[t, place(q, rows, odd), c : c + CHUNK] = value.astype(BF16)
        if i == count - 1:
            pltpu.make_async_copy(stage.at[t], out_ref.at[t], sems.at[t]).start()

    stream(steps, count, lambda t: prefix_ref[t], lambda t, i, slot: entering[cells_of(i)], store)
    for t in range(steps):
        pltpu.make_async_copy(stage.at[t], out_ref.at[t], sems.at[t]).wait()


def spread(chunks, near1, far1, near0, far0, mid, loc1, loc0, keep, prefix, total):
    steps, _, columns, bins = loc1.shape
    rows = keep.shape[0]
    vmem = pl.BlockSpec(memory_space=pltpu.VMEM)
    return pl.pallas_call(
        functools.partial(spread_kernel, chunks, rows),
        out_shape=jax.ShapeDtypeStruct((steps, rows, columns, bins), BF16),
        in_specs=[vmem] * 10,
        out_specs=pl.BlockSpec(memory_space=pl.ANY),
        scratch_shapes=[
            pltpu.VMEM((rows, columns, 2 * bins), BF16),
            pltpu.VMEM((rows, columns, bins), F32),
            pltpu.VMEM((1, columns, bins), F32),
            pltpu.VMEM((1, columns, bins), F32),
            pltpu.VMEM((steps, rows, columns, bins), BF16),
            pltpu.SemaphoreType.DMA((steps,)),
        ],
        compiler_params=pltpu.CompilerParams(vmem_limit_bytes=16 * MIB),
        cost_estimate=pl.CostEstimate(
            flops=8 * steps * rows * columns * bins * bins,
            bytes_accessed=steps * rows * columns * bins * 2,
            transcendentals=0,
        ),
        name="spread",
    )(near1, far1, near0, far0, mid, loc1, loc0, keep, prefix, total)


def local(previous, initial, rates, transitions):
    steps, rows, columns, bins = previous.shape
    strips, blocks = lax.axis_size("space"), lax.axis_size("tm")
    outer_edge, inner_edge = edges(previous, rates)
    between = [(i, i + 1) for i in range(1, strips - 1, 2)]
    within = [(i, i + 1) for i in range(0, strips, 2)]
    outer = lax.ppermute(outer_edge, "space", between + [(j, i) for i, j in between])
    inner = lax.ppermute(inner_edge, "space", within + [(j, i) for i, j in within])

    def send(code, hop):
        return lax.ppermute(code, "tm", [(i, i + hop) for i in range(blocks - hop)])

    most, rest = tuple(range(1, rows)), (0,)
    loc1, code1, part, first, keep, rhs = inner_rows(previous, inner, initial, rates, transitions)
    near1, far1 = send(code1, 1), send(code1, 3)
    loc0, code0, code = outer_row(outer, part, first, keep, rhs, code1)
    mid, near0, far0 = send(code, 2), send(code0, 1), send(code0, 3)
    prefix, total = products(transitions, steps)
    chunks = (most, rest)
    ready1 = ready(most, near1, far1, keep, total)
    return spread(chunks, *ready1, near0, far0, mid, loc1, loc0, keep, prefix, total)


def solution(mesh):
    in_specs = (P("tm", "space", None, None), P("space", None, None), P("space", None), P())
    out_specs = P("tm", "space", None, None)
    return jax.shard_map(local, mesh=mesh, in_specs=in_specs, out_specs=out_specs, check_vma=False)
```
